128 devices in a mesh: row: 8 (over x, core), col: 16 (over z, y).
Axes of the slice: x: 4, y: 4, z: 4, core: 2. Of those that a mesh axis runs over, the one named last changes fastest.
Arguments:
- features: bfloat16 [131072, 128], P(('row', 'col')), may hold values from -6 to 6
- cotangent: bfloat16 [131072, 256], P(('row', 'col')), may hold values from -6 to 6
- w_self: bfloat16 [128, 256], replicated, may hold values from -0.5 to 0.5
- w_neigh: bfloat16 [128, 256], replicated, may hold values from -0.5 to 0.5
- bias: float32 [256], replicated, may hold values from -4 to 4
- src_slot: int32 [1048576], P(('row', 'col')), may hold values from 0 to 2047, as said below
- dst_slot: int32 [1048576], P(('row', 'col')), may hold values from 0 to 2047, as said below
- edge_live: int32 [128], P(('row', 'col')), may hold values from 2048 to 8192, as said below
- mirror_list: int32 [128, 128, 8], P(('row', 'col')), may hold values from -1 to 1023, as said below
Outputs:
- activation: bfloat16 [131072, 256], P(('row', 'col'))
- grad_features: bfloat16 [131072, 128], P(('row', 'col'))
- grad_w_self: float32 [128, 256], replicated
- grad_w_neigh: float32 [128, 256], replicated
- grad_bias: float32 [256], replicated
The draws below stay inside these ranges and needn't reach their ends.
Inputs may be any that keep to these rules, and one draw needn't show every extreme that they name: In each list mirror_list[q, p, :] the entries other than -1 come first, number 1 to 8, and are distinct; some device p receives 8 rows from every device q. `src_slot`: each slot is below 1024 or names a mirror slot 1024 + q * 8 + j of its device p with mirror_list[q, p, j] not -1. `dst_slot`: each slot is below 1024 or names a mirror slot 1024 + q * 8 + j of its device p with mirror_list[q, p, j] not -1. `edge_live`: some device has all 8192 edges live.
All inputs are finite; a program needn't handle non-finite values.
Results may differ from the reference program's by a relative error of at most 0.0075.
Values may be sent and summed in bfloat16 or wider, within the bound.
No kernel may reach another device: no remote copies, remote signals or barrier semaphores. Data moves between devices by JAX's collectives and lax.ppermute only.
A program may use at most 64 MiB of HBM per device.

```python
import jax
import jax.numpy as jnp
from jax import lax

F = 128
H = 256
V_DEV = 1024
E_DEV = 8192
CAP = 8
PEERS = 128
VERTS = 131072
EDGES = 1048576


PRIME_TABLE = (65521, 65519, 65497, 65479, 65449, 65447, 65437, 65423)


def peer_counts(key):
    key = jax.random.fold_in(key, 101)
    first, second = jax.random.split(key)
    base = jax.random.randint(first, (PEERS, PEERS), 1, CAP + 1)
    center = jax.random.randint(second, (), 0, PEERS)
    return jnp.where(jnp.arange(PEERS)[None, :] == center, CAP, base).astype(jnp.int32)


def edge_slots(key, counts):
    parts = jax.random.split(key, 4)
    device = jnp.arange(EDGES, dtype=jnp.int32) // E_DEV
    remote = jax.random.randint(parts[0], (EDGES,), 0, 2)
    own = jax.random.randint(parts[1], (EDGES,), 0, V_DEV)
    peer = jax.random.randint(parts[2], (EDGES,), 0, PEERS)
    spare = jax.random.randint(parts[3], (EDGES,), 0, 1 << 20)
    place = spare % counts[peer, device]
    return jnp.where(remote == 1, V_DEV + peer * CAP + place, own).astype(jnp.int32)


def draw_mirror_list(key, part):
    counts = peer_counts(key)
    key = jax.random.fold_in(key, 7)
    first, second = jax.random.split(key)
    offset = jax.random.randint(first, (PEERS, PEERS, 1), 0, V_DEV)
    pick = jax.random.randint(second, (PEERS, PEERS, 1), 0, len(PRIME_TABLE))
    stride = jnp.array(PRIME_TABLE, jnp.int32)[pick]
    places = jnp.arange(CAP, dtype=jnp.int32)[None, None, :]
    entry = (offset + places * stride) % V_DEV
    return jnp.where(places < counts[:, :, None], entry, -1).astype(jnp.int32)


def draw_src_slot(key, part):
    counts = peer_counts(key)
    key = jax.random.fold_in(key, 11)
    return edge_slots(key, counts)


def draw_dst_slot(key, part):
    counts = peer_counts(key)
    key = jax.random.fold_in(key, 13)
    return edge_slots(key, counts)


def draw_edge_live(key, part):
    key = jax.random.fold_in(key, 17)
    first, second = jax.random.split(key)
    base = jax.random.randint(first, (PEERS,), E_DEV // 4, E_DEV + 1)
    fullest = jax.random.randint(second, (), 0, PEERS)
    return jnp.where(jnp.arange(PEERS) == fullest, E_DEV, base).astype(jnp.int32)


def steps_of(key, dims, pieces, low, high):
    def one(axis_at, blocks):
        steps = jax.random.uniform(jax.random.fold_in(jax.random.fold_in(key, 6), axis_at), (blocks,), jnp.float32, low / len(pieces), high / len(pieces))
        return jnp.repeat(jnp.exp(steps), dims[axis_at] // blocks).reshape((-1,) + (1,) * (len(dims) - axis_at - 1))

    gain = one(*pieces[0])
    for cut in pieces[1:]:
        gain = gain * one(*cut)
    return gain


def noise(rng, shape, width, bound, shards=(), held_as=jnp.bfloat16):
    entries = width * jax.random.normal(rng, shape, jnp.float32)
    if shards:
        entries = entries * steps_of(rng, shape, shards, -0.22, 0.18)
    return jnp.clip(entries, -bound, bound).astype(held_as)


def setup_inputs(seed: int = 0) -> dict:
    arg_keys = jax.random.split(jax.random.key(seed), 10)
    features = noise(arg_keys[0], (VERTS, F), 1.0, 6.0, ((0, 128),))
    cotangent = noise(arg_keys[1], (VERTS, H), 1.0, 6.0, ((0, 128),))
    w_self = noise(arg_keys[2], (F, H), F ** -0.5, 0.5)
    w_neigh = noise(arg_keys[3], (F, H), F ** -0.5, 0.5)
    bias = noise(arg_keys[4], (H,), 0.7, 4.0, (), jnp.float32)
    src_slot = draw_src_slot(jax.random.fold_in(arg_keys[9], 71), 0)
    dst_slot = draw_dst_slot(jax.random.fold_in(arg_keys[9], 71), 0)
    edge_live = draw_edge_live(jax.random.fold_in(arg_keys[9], 71), 0)
    mirror_list = draw_mirror_list(jax.random.fold_in(arg_keys[9], 71), 0)
    return dict(features=features, cotangent=cotangent, w_self=w_self, w_neigh=w_neigh, bias=bias, src_slot=src_slot, dst_slot=dst_slot, edge_live=edge_live, mirror_list=mirror_list)


def spread_add(source, take, put, weights, verts):
    def step(total, block):
        picks, places, scale = block
        rows = source[picks].astype(jnp.float32) * scale[:, None]
        return total.at[places].add(rows), None
    start = jnp.zeros((verts, source.shape[1]), jnp.float32)
    total, _ = lax.scan(step, start, (take, put, weights))
    return total


def reference(features, cotangent, w_self, w_neigh, bias, src_slot, dst_slot, edge_live, mirror_list):
    verts = PEERS * V_DEV
    lists = jnp.transpose(mirror_list, (1, 0, 2))
    anchor = (jnp.arange(PEERS, dtype=jnp.int32) * V_DEV)[None, :, None]
    mirror_ids = jnp.where(lists >= 0, anchor + lists, 0).astype(jnp.int32).reshape(PEERS, PEERS * CAP)
    own_ids = (jnp.arange(PEERS, dtype=jnp.int32)[:, None] * V_DEV + jnp.arange(V_DEV, dtype=jnp.int32)[None, :]).astype(jnp.int32)
    slot_ids = jnp.concatenate([own_ids, mirror_ids], axis=1)
    src_ids = jnp.take_along_axis(slot_ids, src_slot.reshape(PEERS, E_DEV), axis=1)
    dst_ids = jnp.take_along_axis(slot_ids, dst_slot.reshape(PEERS, E_DEV), axis=1)
    live = (jnp.arange(E_DEV, dtype=jnp.int32)[None, :] < edge_live[:, None]).astype(jnp.float32)
    sums = spread_add(features, src_ids, dst_ids, live, verts)
    degree = jnp.zeros((verts,), jnp.float32).at[dst_ids.reshape(-1)].add(live.reshape(-1))
    inverse = 1.0 / jnp.maximum(degree, 1.0)
    aggregate = (sums * inverse[:, None]).astype(jnp.bfloat16)
    pre = jnp.dot(features, w_self, preferred_element_type=jnp.float32) + jnp.dot(aggregate, w_neigh, preferred_element_type=jnp.float32) + bias
    sig = jax.nn.sigmoid(pre)
    activation = (pre * sig).astype(jnp.bfloat16)
    grad_pre = (cotangent.astype(jnp.float32) * sig * (1.0 + pre * (1.0 - sig))).astype(jnp.bfloat16)
    grad_w_self = jnp.dot(features.T, grad_pre, preferred_element_type=jnp.float32)
    grad_w_neigh = jnp.dot(aggregate.T, grad_pre, preferred_element_type=jnp.float32)
    grad_bias = jnp.sum(grad_pre.astype(jnp.float32), axis=0)
    message = (jnp.dot(grad_pre, w_neigh.T, preferred_element_type=jnp.float32) * inverse[:, None]).astype(jnp.bfloat16)
    spread = spread_add(message, dst_ids, src_ids, live, verts)
    grad_features = (jnp.dot(grad_pre, w_self.T, preferred_element_type=jnp.float32) + spread).astype(jnp.bfloat16)
    return activation, grad_features, grad_w_self, grad_w_neigh, grad_bias
```

```python
import jax
import jax.numpy as jnp
from jax import lax
from jax.experimental import pallas as pl
from jax.experimental.pallas import tpu as pltpu
from jax.sharding import PartitionSpec as P

F32 = jnp.float32
BF16 = jnp.bfloat16
AXES = ("row", "col")

MASTERS = 1024
MIRRORS = 1024
SLOTS = MASTERS + MIRRORS
EDGES = 8192
PEERS = 128
F = 128
H = 256
LANES = 128
COPIES = 4
TURN = 64
WORDS = SLOTS * (SLOTS // 512)


def dot(a, b):
    return jnp.dot(a, b, preferred_element_type=F32)


def dot_nt(a, b):
    return lax.dot_general(a, b, (((1,), (1,)), ((), ())), preferred_element_type=F32)


def dot_tn(a, b):
    return lax.dot_general(a, b, (((0,), (0,)), ((), ())), preferred_element_type=F32)


def gather_matrix(column):
    places = lax.broadcasted_iota(jnp.int32, (MIRRORS, MASTERS), 1)
    return jnp.where(places == column, 1.0, 0.0).astype(BF16)


def scatter_matrix(line):
    places = lax.broadcasted_iota(jnp.int32, (MASTERS, MIRRORS), 0)
    return jnp.where(places == line, 1.0, 0.0).astype(BF16)


def pull_kernel(column_ref, rows_ref, out_ref):
    picked = dot(gather_matrix(column_ref[...]), rows_ref[...])
    out_ref[...] = picked.reshape(PEERS, 8, F).astype(BF16)


def build_kernel(live_ref, place_ref, lane_ref, rows_ref, a_ref, part_ref, hot3, *tables3):
    hot = hot3.reshape(4 * LANES, LANES)
    tables = [t.reshape(WORDS, LANES) for t in tables3]
    r = lax.broadcasted_iota(jnp.int32, (4 * LANES, LANES), 0)
    c = lax.broadcasted_iota(jnp.int32, (4 * LANES, LANES), 1)
    value = jnp.zeros((4 * LANES, LANES), jnp.int32)
    for q in range(4):
        value = jnp.where(r == c + LANES * q, 1 << (8 * q), value)
    hot[...] = value

    def clear(i, carry):
        for t in tables:
            t[pl.ds(pl.multiple_of(i * 256, 256), 256), :] = jnp.zeros((256, LANES), jnp.int32)
        return carry

    lax.fori_loop(0, WORDS // 256, clear, 0)
    n = live_ref[0]

    def turn(i, carry):
        for g in range(TURN // COPIES):
            at = [pl.ds(g * COPIES + k, EDGES - TURN + 1) for k in range(COPIES)]
            where = [place_ref.at[s][i * TURN] for s in at]
            hots = [hot3[lane_ref.at[s][i * TURN]] for s in at]
            olds = [tables3[k][where[k]] for k in range(COPIES)]
            for k in range(COPIES):
                tables3[k][where[k]] = olds[k] + hots[k]
        return carry

    turns = n // TURN
    lax.fori_loop(0, turns, turn, 0)

    def rest(e, carry):
        tables3[0][place_ref[e]] = tables3[0][place_ref[e]] + hot3[lane_ref[e]]
        return carry

    lax.fori_loop(turns * TURN, n, rest, 0)

    ones = jnp.ones((MASTERS, LANES), BF16)
    wide = jnp.concatenate([rows_ref[...], ones], axis=1)

    def widen(read, carry):
        def block(i, carry):
            d = pl.multiple_of(i * 128, 128)
            for j in range(4):
                for q, counts in enumerate(read(pl.ds(pl.multiple_of(j * SLOTS + d, 128), 128))):
                    left = q * 512 + j * LANES
                    a_ref[pl.ds(d, 128), left : left + LANES] = counts.astype(F32).astype(BF16)
            own = dot(a_ref[pl.ds(d, 128), :MASTERS], wide)
            far = dot(a_ref[pl.ds(d, 128), MASTERS:], ones)
            part_ref[pl.ds(d, 128), :F] = own[:, :F]
            part_ref[pl.ds(d, 128), F:] = own[:, F:] + far
            return carry

        return lax.fori_loop(0, SLOTS // 128, block, carry)

    def read_bytes(at):
        x = tables[0][at, :]
        for t in tables[1:]:
            x = x + t[at, :]
        yield x & 255
        for q in range(1, 4):
            yield lax.shift_right_logical(x, 8 * q) & 255

    widen(read_bytes, 0)

    found = jnp.sum(part_ref[:, F : F + 1])

    @pl.when(found != n.astype(F32))
    def _():
        lax.fori_loop(0, WORDS // 256, clear, 0)

        def edge(e, carry):
            at = place_ref[e]
            lane = lane_ref[e]
            q = lane // LANES
            one = jnp.where(
                lax.broadcasted_iota(jnp.int32, (1, LANES), 1) == lane % LANES,
                jnp.where(q % 2 == 1, 65536, 1),
                0,
            )
            tables3[0][at] = tables3[0][at] + jnp.where(q < 2, one, 0)
            tables3[1][at] = tables3[1][at] + jnp.where(q < 2, 0, one)
            return carry

        lax.fori_loop(0, n, edge, 0)

        def read_halves(at):
            for t in tables[:2]:
                x = t[at, :]
                yield x & 65535
                yield lax.shift_right_logical(x, 16)

        widen(read_halves, 0)


def split(x):
    high = x.astype(BF16).astype(F32)
    return high, (x - high).astype(BF16).astype(F32)


def low_half(shape):
    return lax.broadcasted_iota(jnp.int32, shape, len(shape) - 1) < shape[-1] // 2


def push_kernel(a_ref, part_ref, got_ref, out_ref):
    rows = got_ref[...].reshape(MIRRORS, F)
    sums = part_ref[:, :F] + dot(a_ref[...], rows)
    high, low = split(part_ref[:, F:])
    tally = jnp.where(low_half((MIRRORS, LANES)), high, low)
    both = jnp.concatenate([sums.reshape(PEERS, 8, F), tally.reshape(PEERS, 8, F)], axis=1)
    out_ref[...] = both.astype(BF16)


def local_kernel(a_ref, part_ref, got_ref, rows_ref, w_ref, bias_ref, part_out, pre_out):
    part_out[:, :F] = part_ref[:, :F] + dot(a_ref[...], got_ref[...].reshape(MIRRORS, F))
    part_out[:, F:] = part_ref[:, F:]
    pre_out[...] = dot(rows_ref[...], w_ref[...]) + bias_ref[...]


def dense_kernel(
    got_ref, part_ref, pre_ref, line_ref, column_ref, rows_ref, w_ref, cot_ref,
    act_ref, grad_ref, msg_ref, out_ref, bias_ref,
):
    got = got_ref[...].astype(F32)
    wide = jnp.concatenate(
        [got[:, :8].reshape(MIRRORS, F), got[:, 8:].reshape(MIRRORS, LANES)], axis=1
    ).astype(BF16)
    folded = dot(scatter_matrix(line_ref[...]), wide)
    tally = folded[:, F:]
    degree = part_ref[:, F:] + (tally + pltpu.roll(tally, LANES // 2, 1))
    inverse = 1.0 / jnp.maximum(degree, 1.0)
    aggregate = ((part_ref[:, :F] + folded[:, :F]) * inverse).astype(BF16)
    w = w_ref[...]
    pre = pre_ref[...] + dot(aggregate, w)
    sig = jax.nn.sigmoid(pre)
    act_ref[...] = (pre * sig).astype(BF16)
    grad = (cot_ref[...].astype(F32) * sig * (1.0 + pre * (1.0 - sig))).astype(BF16)
    grad_ref[...] = grad
    msg = (dot_nt(grad, w) * inverse).astype(BF16)
    msg_ref[...] = msg
    picked = dot(gather_matrix(column_ref[...]), msg).reshape(PEERS, 8, F)
    terms = dot_tn(jnp.concatenate([rows_ref[...], aggregate], axis=1), grad)
    flat = jnp.concatenate([terms[:, :F], terms[:, F:]], axis=0).reshape(PEERS // 2, 8, F)
    high, low = split(flat)
    first = lax.broadcasted_iota(jnp.int32, (PEERS // 2, 8, F), 1) < 4
    even = jnp.where(first, high, pltpu.roll(low, 4, 1))
    odd = jnp.where(first, pltpu.roll(high, 4, 1), low)
    mixed = jnp.stack([even, odd], axis=1).reshape(PEERS, 8, F)
    out_ref[...] = jnp.concatenate([picked, mixed], axis=1).astype(BF16)
    total = dot(jnp.ones((8, MASTERS), BF16), grad)
    high, low = split(total)
    sub = lax.broadcasted_iota(jnp.int32, (8, F), 0)
    tile = jnp.where(sub == 4, high[:, :F], 0.0)
    tile = jnp.where(sub == 5, high[:, F:], tile)
    tile = jnp.where(sub == 6, low[:, :F], tile)
    bias_ref[...] = jnp.where(sub == 7, low[:, F:], tile)


def back_local_kernel(a_ref, msg_ref, grad_ref, w_ref, base_ref, mirror_ref):
    spread = dot_tn(msg_ref[...], a_ref[...])
    base_ref[...] = spread[:, :MASTERS].T + dot_nt(grad_ref[...], w_ref[...])
    mirror_ref[...] = spread[:, MASTERS:]


def back_push_kernel(a_ref, mirror_ref, got_ref, bias_ref, out_ref):
    got = got_ref[...].astype(F32)
    rows = got[:, :8].reshape(MIRRORS, F).astype(BF16)
    spread = (mirror_ref[...] + dot_tn(rows, a_ref[...])).T
    total = jnp.sum(got[:, 8:], axis=0)
    total = total + pltpu.roll(total, 4, 0)
    sub = lax.broadcasted_iota(jnp.int32, (8, F), 0)
    tile = jnp.where(sub < 4, total, bias_ref[...])
    tile = jnp.broadcast_to(tile[None], (PEERS, 8, F))
    both = jnp.concatenate([spread.reshape(PEERS, 8, F), tile], axis=1)
    out_ref[...] = both.astype(BF16)


def back_mirror_kernel(a_ref, base_ref, got_ref, out_ref):
    got = got_ref[...].astype(F32)
    rows = got[:, :8].reshape(MIRRORS, F).astype(BF16)
    out_ref[...] = base_ref[...] + dot_tn(rows, a_ref[...]).T


def last_kernel(base_ref, got_ref, line_ref, grad_ref, self_ref, neigh_ref, bias_ref):
    got = got_ref[...].astype(F32)
    rows = got[:, :8].reshape(MIRRORS, F).astype(BF16)
    grad_ref[...] = (base_ref[...] + dot(scatter_matrix(line_ref[...]), rows)).astype(BF16)
    tiles = got[:, 8:]
    pairs = tiles.reshape(PEERS // 2, 2, 8, F)
    first = lax.broadcasted_iota(jnp.int32, (PEERS // 2, 8, F), 1) < 4
    flat = jnp.where(first, pairs[:, 0], pltpu.roll(pairs[:, 1], 4, 1)).reshape(2 * H, F)
    self_ref[:, :F] = flat[:F]
    self_ref[:, F:] = flat[H : H + F]
    neigh_ref[:, :F] = flat[F:H]
    neigh_ref[:, F:] = flat[H + F :]
    total = jnp.sum(tiles, axis=0)
    bias_ref[...] = total + pltpu.roll(total, 6, 0)


def vmem(shape=None, index=None):
    if shape is None:
        return pl.BlockSpec(memory_space=pltpu.VMEM)
    return pl.BlockSpec(shape, lambda i: index, memory_space=pltpu.VMEM, pipeline_mode=pl.Buffered(1))


def call(kernel, ins, outs, specs, name, mib=32, scratch=(), flops=0, moved=0):
    return pl.pallas_call(
        kernel,
        grid=(1,),
        out_shape=[jax.ShapeDtypeStruct(s, t) for s, t in outs],
        in_specs=specs,
        out_specs=[vmem() for _ in outs],
        scratch_shapes=list(scratch),
        compiler_params=pltpu.CompilerParams(vmem_limit_bytes=mib * 1024 * 1024),
        cost_estimate=pl.CostEstimate(flops=flops, bytes_accessed=moved, transcendentals=0),
        name=name,
    )(*ins)


def exchange(x):
    return lax.all_to_all(x, AXES, split_axis=0, concat_axis=0, tiled=True)


def local(features, cotangent, w_self, w_neigh, bias, src_slot, dst_slot, edge_live, mirror_list):
    line = mirror_list.reshape(1, MIRRORS)
    column = mirror_list.reshape(MIRRORS, 1)
    place = ((src_slot >> 7) & 3) * SLOTS + dst_slot
    lane = (src_slot & 127) | ((src_slot >> 9) << 7)
    smem = pl.BlockSpec(memory_space=pltpu.SMEM)
    corner = {
        (i, j): vmem((1024, 1024), (i, j)) for i in range(2) for j in range(2)
    }

    (out1,) = call(
        pull_kernel, (column, features), [((PEERS, 8, F), BF16)], [vmem()] * 2, "pull"
    )
    got1 = exchange(out1)

    a, part = call(
        build_kernel,
        (edge_live, place, lane, features),
        [((SLOTS, SLOTS), BF16), ((SLOTS, 2 * F), F32)],
        [smem, smem, smem, vmem()],
        "build",
        mib=40,
        scratch=[pltpu.VMEM((4 * LANES, 1, LANES), jnp.int32)]
        + [pltpu.VMEM((WORDS, 1, LANES), jnp.int32) for _ in range(COPIES)],
        flops=20_000_000_000,
        moved=20_000_000,
    )
    (out2,) = call(
        push_kernel,
        (a, part, got1),
        [((PEERS, 16, F), BF16)],
        [corner[1, 1], vmem((1024, 2 * F), (1, 0)), vmem()],
        "push",
    )
    got2 = exchange(out2)
    part_m, pre = call(
        local_kernel,
        (a, part, got1, features, w_self, bias.reshape(1, H)),
        [((MASTERS, 2 * F), F32), ((MASTERS, H), F32)],
        [corner[0, 1], vmem((1024, 2 * F), (0, 0)), vmem(), vmem(), vmem(), vmem()],
        "local",
        flops=2_000_000_000,
        moved=6_000_000,
    )
    act, grad, msg, out3, bias_tile = call(
        dense_kernel,
        (got2, part_m, pre, line, column, features, w_neigh, cotangent),
        [
            ((MASTERS, H), BF16),
            ((MASTERS, H), BF16),
            ((MASTERS, F), BF16),
            ((PEERS, 16, F), BF16),
            ((8, F), F32),
        ],
        [vmem()] * 8,
        "dense",
    )
    got3 = exchange(out3)
    base, mirror = call(
        back_local_kernel,
        (a, msg, grad, w_self),
        [((MASTERS, F), F32), ((F, MIRRORS), F32)],
        [vmem((1024, 2048), (0, 0)), vmem(), vmem(), vmem()],
        "back_local",
        flops=2_000_000_000,
        moved=6_000_000,
    )
    (out4,) = call(
        back_push_kernel,
        (a, mirror, got3, bias_tile),
        [((PEERS, 16, F), BF16)],
        [corner[1, 1], vmem(), vmem(), vmem()],
        "back_push",
    )
    got4 = exchange(out4)
    (base2,) = call(
        back_mirror_kernel,
        (a, base, got3),
        [((MASTERS, F), F32)],
        [corner[1, 0], vmem(), vmem()],
        "back_mirror",
        flops=2_000_000_000,
        moved=6_000_000,
    )
    grad_features, grad_self, grad_neigh, bias_out = call(
        last_kernel,
        (base2, got4, line),
        [((MASTERS, F), BF16), ((F, H), F32), ((F, H), F32), ((8, F), F32)],
        [vmem()] * 3,
        "last",
    )
    return act, grad_features, grad_self, grad_neigh, bias_out[4:6].reshape(H)


def solution(mesh):
    placed = (
        P(AXES, None),
        P(AXES, None),
        P(),
        P(),
        P(),
        P(AXES),
        P(AXES),
        P(AXES),
        P(AXES, None, None),
    )
    return jax.shard_map(
        local,
        mesh=mesh,
        in_specs=placed,
        out_specs=(P(AXES, None), P(AXES, None), P(), P(), P()),
        check_vma=False,
    )
```

```python
import jax
import jax.numpy as jnp
from jax import lax
from jax.experimental import pallas as pl
from jax.experimental.pallas import tpu as pltpu
from jax.sharding import PartitionSpec as P

F32 = jnp.float32
BF16 = jnp.bfloat16
AXES = ("row", "col")

MASTERS = 1024
MIRRORS = 1024
SLOTS = MASTERS + MIRRORS
EDGES = 8192
PEERS = 128
F = 128
H = 256
LANES = 128
COPIES = 6
TURN = 128
PARTS = 4
WORDS = SLOTS * (SLOTS // 512)


def part_of(size, k):
    return pl.ds(k * (size // PARTS), size // PARTS)


def dot(a, b):
    return jnp.dot(a, b, preferred_element_type=F32)


def dot_nt(a, b):
    return lax.dot_general(a, b, (((1,), (1,)), ((), ())), preferred_element_type=F32)


def gather_matrix(column):
    places = lax.broadcasted_iota(jnp.int32, (MIRRORS, MASTERS), 1)
    return jnp.where(places == column, 1.0, 0.0).astype(BF16)


def scatter_matrix(line):
    places = lax.broadcasted_iota(jnp.int32, (MASTERS, MIRRORS), 0)
    return jnp.where(places == line, 1.0, 0.0).astype(BF16)


def as_column(lists):
    turned = jnp.transpose(lists.astype(F32))
    shape = (PEERS, 8, 8)
    spread = jnp.broadcast_to(turned[:, None, :], shape)
    here = lax.broadcasted_iota(jnp.int32, shape, 1) == lax.broadcasted_iota(jnp.int32, shape, 2)
    column = jnp.sum(jnp.where(here, spread, 0.0), axis=2, keepdims=True)
    return column.reshape(MIRRORS, 1).astype(jnp.int32)


def pull_kernel(lists_ref, rows_ref, out_ref):
    matrix = gather_matrix(as_column(lists_ref[...]))
    rows = rows_ref[...]
    for c in range(2):
        picked = dot(matrix[c * 512 : (c + 1) * 512], rows).reshape(PEERS // 2, 8, F)
        half = pl.ds(c * (PEERS // 2), PEERS // 2)
        out_ref[half] = picked.astype(BF16)
        out_ref.send(half)


def build_kernel(
    live_ref, src_ref, dst_ref, rows_ref, mm_ref, mg_ref, gm_ref, gg_ref, sums_ref, tally_ref,
    code_ref, codes, sem, *tables3
):
    tables = [t.reshape(WORDS, LANES) for t in tables3]
    n = live_ref[0]

    def clear(i, carry):
        for t in tables:
            t[pl.ds(pl.multiple_of(i * 256, 256), 256), :] = jnp.zeros((256, LANES), jnp.int32)
        return carry

    lax.fori_loop(0, WORDS // 512, clear, 0)
    src, dst = src_ref[...], dst_ref[...]
    shape = (EDGES // LANES, LANES)
    number = lax.broadcasted_iota(jnp.int32, shape, 0) * LANES
    number = number + lax.broadcasted_iota(jnp.int32, shape, 1)
    place = ((src >> 7) & 3) * SLOTS + dst
    code = place | ((src & 127) << 13) | ((src >> 9) << 24)
    code_ref[...] = jnp.where(number < n, code, 128 << 13)
    move = pltpu.make_async_copy(code_ref, codes, sem)
    move.start()
    lax.fori_loop(WORDS // 512, WORDS // 256, clear, 0)
    move.wait()

    lanes = lax.broadcasted_iota(jnp.int32, (1, LANES), 1) << 13
    one = jnp.ones((1, LANES), jnp.int32)

    def turn(i, carry):
        for start in range(0, TURN, COPIES):
            count = min(COPIES, TURN - start)
            words = [codes[i, start + k] for k in range(count)]
            where = [w & (WORDS - 1) for w in words]
            adds = []
            for w in words:
                w = jnp.full((1, LANES), w, jnp.int32)
                bit = lax.shift_left(one, lax.shift_right_logical(w, 21))
                adds.append(jnp.where(lanes == (w & (255 << 13)), bit, 0))
            olds = [tables3[k][where[k]] for k in range(count)]
            for k in range(count):
                tables3[k][where[k]] = olds[k] + adds[k]
        return carry

    turns = (n + TURN - 1) // TURN
    lax.fori_loop(0, turns, turn, 0)

    def put(near_ref, far_ref, to, at, read, seen):
        for j in range(4):
            words = read(pl.ds(pl.multiple_of(j * SLOTS + at, 128), 128))
            for q, counts in enumerate(words):
                half = near_ref if q < 2 else far_ref
                left = (q % 2) * 512 + j * LANES
                half[pl.ds(to, 128), pl.ds(left, LANES)] = counts.astype(F32).astype(BF16)
                seen = seen + jnp.sum(counts.reshape(16, 8, LANES), axis=0)
        return seen

    ones = jnp.ones((MASTERS, LANES), BF16)
    wide = jnp.concatenate([rows_ref[...], ones], axis=1)

    def widen(read):
        def mirrors(i, seen):
            d = pl.multiple_of(i * 128, 128)
            return put(gm_ref, gg_ref, d, MASTERS + d, read, seen)

        def masters(i, seen):
            e = pl.multiple_of(i * 256, 256)
            own = dot(gm_ref[pl.ds(e, 256), :], wide)
            far = dot(gg_ref[pl.ds(e, 256), :], ones)
            sums_ref[pl.ds(e, 256), :] = own[:, :F]
            tally_ref[pl.ds(e, 256), :] = two_parts(own[:, F:] + far)
            for h in range(2):
                d = pl.multiple_of(i * 256 + h * 128, 128)
                seen = put(mm_ref, mg_ref, d, d, read, seen)
            mm_ref.send(pl.ds(e, 256))
            mg_ref.send(pl.ds(e, 256))
            return seen

        seen = lax.fori_loop(0, MIRRORS // 128, mirrors, jnp.zeros((8, LANES), jnp.int32))
        gg_ref.send()
        gm_ref.send()
        seen = lax.fori_loop(0, MASTERS // 256, masters, seen)
        sums_ref.send()
        tally_ref.send()
        return seen

    def finish():
        for ref in (mm_ref, mg_ref, gm_ref, gg_ref, sums_ref, tally_ref):
            ref.wait()

    def read_bytes(at):
        x = tables[0][at, :]
        for t in tables[1:]:
            x = x + t[at, :]
        yield x & 255
        yield lax.shift_right_logical(x, 8) & 255
        yield lax.shift_right_logical(x, 16) & 255
        yield lax.shift_right_logical(x, 24)

    found = jnp.sum(widen(read_bytes).astype(F32))
    finish()

    @pl.when(found != n.astype(F32))
    def _():
        lax.fori_loop(0, WORDS // 256, clear, 0)

        def edge(e, carry):
            word = codes[e // LANES, e % LANES]
            at = word & (WORDS - 1)
            q = word >> 24
            one = jnp.where(
                lanes == (word & (127 << 13)), jnp.where(q % 2 == 1, 65536, 1), 0
            )
            tables3[0][at] = tables3[0][at] + jnp.where(q < 2, one, 0)
            tables3[1][at] = tables3[1][at] + jnp.where(q < 2, 0, one)
            return carry

        lax.fori_loop(0, n, edge, 0)

        def read_halves(at):
            for t in tables[:2]:
                x = t[at, :]
                yield x & 65535
                yield lax.shift_right_logical(x, 16)

        widen(read_halves)
        finish()


def split(x):
    high = x.astype(BF16).astype(F32)
    return high, (x - high).astype(BF16).astype(F32)


def two_parts(x):
    high, low = split(x)
    left = lax.broadcasted_iota(jnp.int32, x.shape, 1) < LANES // 2
    return jnp.where(left, high, low).astype(BF16)


def push_kernel(got_ref, sums_ref, gg_ref, tally_ref, out_ref):
    got = got_ref[...].reshape(MIRRORS, F)
    for c in range(PARTS):
        rows, peers = part_of(MIRRORS, c), part_of(PEERS, c)
        sums = dot(gg_ref.part(c), got) + sums_ref[rows]
        tally = tally_ref[rows].astype(F32)
        shape = (PEERS // PARTS, 8, F)
        both = jnp.concatenate([sums.reshape(shape), tally.reshape(shape)], axis=1)
        out_ref[peers] = both.astype(BF16)
        out_ref.send(peers)


def local_kernel(
    rows_ref, lists_ref, mm_ref, got_ref, mg_ref, gather_ref, turned_ref, sums_ref, tally_ref
):
    gather_ref[...] = gather_matrix(as_column(lists_ref[...]))
    gather_ref.send()
    rows = rows_ref[...]
    turned_ref[...] = rows.astype(F32).T.astype(BF16)
    turned_ref.send()
    ones = jnp.ones((MASTERS, LANES), BF16)
    got = got_ref[...].reshape(MIRRORS, F)
    both = dot(mm_ref[...], jnp.concatenate([rows, ones], axis=1)) + dot(
        mg_ref[...], jnp.concatenate([got, ones], axis=1)
    )
    sums_ref[...] = both[:, :F]
    sums_ref.send()
    tally_ref[...] = two_parts(both[:, F:])
    tally_ref.send()


def dense_kernel(
    line_ref, got_ref, tally_ref, sums_ref, self_ref, bias_ref, rows_ref, neigh_ref, cot_ref,
    gather_ref, turned_ref,
    act_ref, grad_ref, msg_ref, out_ref, total_ref,
):
    scatter = scatter_matrix(line_ref[...])
    got = got_ref[...].astype(F32)
    wide = jnp.concatenate(
        [got[:, :8].reshape(MIRRORS, F), got[:, 8:].reshape(MIRRORS, LANES)], axis=1
    ).astype(BF16)
    folded = dot(scatter, wide)
    tally = folded[:, F:] + tally_ref[...].astype(F32)
    degree = tally + pltpu.roll(tally, LANES // 2, 1)
    inverse = 1.0 / jnp.maximum(degree, 1.0)
    mean = (sums_ref[...] + folded[:, :F]) * inverse
    w = neigh_ref[...]
    pre = dot(rows_ref[...], self_ref[...]) + dot(mean.astype(BF16), w) + bias_ref[...]
    sig = jax.nn.sigmoid(pre)
    act_ref[...] = (pre * sig).astype(BF16)
    act_ref.send()
    grad = (cot_ref[...].astype(F32) * sig * (1.0 + pre * (1.0 - sig))).astype(BF16)
    grad_ref[...] = grad
    grad_ref.send()
    msg = (dot_nt(grad, w) * inverse).astype(BF16)
    msg_ref[...] = msg
    msg_ref.send()
    picked = dot(gather_ref[...], msg).reshape(PEERS, 8, F)
    turned = jnp.concatenate([turned_ref[...], mean.T.astype(BF16)], axis=0)
    terms = dot(turned, grad)
    flat = jnp.concatenate([terms[:, :F], terms[:, F:]], axis=0).reshape(PEERS // 2, 8, F)
    high, low = split(flat)
    first = lax.broadcasted_iota(jnp.int32, (PEERS // 2, 8, F), 1) < 4
    even = jnp.where(first, high, pltpu.roll(low, 4, 1))
    odd = jnp.where(first, pltpu.roll(high, 4, 1), low)
    mixed = jnp.stack([even, odd], axis=1).reshape(PEERS, 8, F)
    out_ref[...] = jnp.concatenate([picked, mixed], axis=1).astype(BF16)
    out_ref.send()
    total = dot(jnp.ones((8, MASTERS), BF16), grad)
    high, low = split(total)
    sub = lax.broadcasted_iota(jnp.int32, (8, F), 0)
    tile = jnp.where(sub == 4, high[:, :F], 0.0)
    tile = jnp.where(sub == 5, high[:, F:], tile)
    tile = jnp.where(sub == 6, low[:, :F], tile)
    total_ref[...] = jnp.where(sub == 7, low[:, F:], tile)
    total_ref.send()


def back_local_kernel(
    gg_ref, msg_ref, mg_ref, mm_ref, grad_ref, w_ref, _, turned_ref, mirror_ref, base_ref
):
    turned_ref[...] = gg_ref[...].T
    turned_ref.send()
    msg = msg_ref[...].astype(F32).T.astype(BF16)
    mirror_ref[...] = dot(msg, mg_ref[...]).T
    mirror_ref.send()
    base_ref[...] = dot(msg, mm_ref[...]).T + dot_nt(grad_ref[...], w_ref[...])
    base_ref.send()


def back_push_kernel(got_ref, mirror_ref, total_ref, turned_ref, out_ref):
    got = got_ref[...].astype(F32)
    rows = got[:, :8].reshape(MIRRORS, F).astype(BF16)
    total = jnp.sum(got[:, 8:], axis=0)
    total = total + pltpu.roll(total, 4, 0)
    sub = lax.broadcasted_iota(jnp.int32, (8, F), 0)
    tile = jnp.where(sub < 4, total, total_ref[...])
    shape = (PEERS // PARTS, 8, F)
    tiles = jnp.broadcast_to(tile[None], shape)
    for c in range(PARTS):
        peers = part_of(PEERS, c)
        spread = dot(turned_ref.part(c), rows) + mirror_ref[part_of(MIRRORS, c)]
        out_ref[peers] = jnp.concatenate([spread.reshape(shape), tiles], axis=1).astype(BF16)
        out_ref.send(peers)


def back_mirror_kernel(got_ref, gm_ref, base_ref, out_ref):
    turned = got_ref[...].astype(F32)[:, :8].reshape(MIRRORS, F).T.astype(BF16)
    out_ref[...] = dot(turned, gm_ref[...]).T + base_ref[...]
    out_ref.send()


def last_kernel(line_ref, got_ref, base_ref, grad_ref, self_ref, neigh_ref, bias_ref):
    got = got_ref[...].astype(F32)
    rows = got[:, :8].reshape(MIRRORS, F).astype(BF16)
    grad_ref[...] = (dot(scatter_matrix(line_ref[...]), rows) + base_ref[...]).astype(BF16)
    grad_ref.send()
    tiles = got[:, 8:]
    pairs = tiles.reshape(PEERS // 2, 2, 8, F)
    first = lax.broadcasted_iota(jnp.int32, (PEERS // 2, 8, F), 1) < 4
    flat = jnp.where(first, pairs[:, 0], pltpu.roll(pairs[:, 1], 4, 1)).reshape(2 * H, F)
    self_ref[:, :F] = flat[:F]
    self_ref[:, F:] = flat[H : H + F]
    neigh_ref[:, :F] = flat[F:H]
    neigh_ref[:, F:] = flat[H + F :]
    total = jnp.sum(tiles, axis=0)
    bias_ref[...] = total[4:6] + total[6:8]
    for ref in (self_ref, neigh_ref, bias_ref):
        ref.send()


VMEM = pl.BlockSpec(memory_space=pltpu.VMEM)
SMEM = pl.BlockSpec(memory_space=pltpu.SMEM)
HBM = pl.BlockSpec(memory_space=pltpu.HBM)
ALL = 60 * 1024 * 1024
NEAR = 55_800_000


class Loaded:
    def __init__(self, source, held, sems, first, parts):
        size = held.shape[0] // parts
        self.held, self.size = held, size
        self.copies = []
        for k in range(parts):
            rows = pl.ds(k * size, size)
            copy = pltpu.make_async_copy(source.at[rows], held.at[rows], sems.at[first + k])
            copy.start()
            self.copies.append(copy)

    def part(self, k):
        if self.copies[k] is not None:
            self.copies[k].wait()
            self.copies[k] = None
        return self.held[pl.ds(k * self.size, self.size)]

    def wait(self):
        for k, copy in enumerate(self.copies):
            if copy is not None:
                copy.wait()
                self.copies[k] = None

    def __getitem__(self, at):
        self.wait()
        return self.held[at]


class Stored:
    def __init__(self, held, target, sem):
        self.held, self.target, self.sem = held, target, sem
        self.copy = pltpu.make_async_copy(held, target, sem)
        self.waited = False

    def __setitem__(self, at, value):
        self.held[at] = value

    def __getitem__(self, at):
        return self.held[at]

    def wait(self):
        self.copy.wait()
        self.waited = True

    def send(self, rows=None):
        if rows is None:
            self.copy.start()
        else:
            pltpu.make_async_copy(self.held.at[rows], self.target.at[rows], self.sem).start()


def call(kernel, ins, outs, name, near=(), scalars=(), scratch=(), parts=None, idle=(), flops=0, moved=0):
    parts = parts or {}
    far = [k for k in range(len(ins)) if k not in (*near, *scalars, *idle)]
    specs = [VMEM if k in near else SMEM if k in scalars else HBM for k in range(len(ins))]
    held = [pltpu.VMEM(ins[k].shape, ins[k].dtype) for k in far]
    held += [pltpu.VMEM(s, t) for s, t in outs]
    counts = [parts.get(k, 1) for k in far]
    dma = pltpu.SemaphoreType.DMA

    def body(*refs):
        operands, refs = list(refs[: len(ins)]), refs[len(ins) :]
        targets, refs = refs[: len(outs)], refs[len(outs) :]
        copies, refs = refs[: len(far)], refs[len(far) :]
        results, refs = refs[: len(outs)], refs[len(outs) :]
        load_sems, store_sems = refs[0], refs[1]
        first = 0
        for k, copy, count in zip(far, copies, counts, strict=True):
            operands[k] = Loaded(operands[k], copy, load_sems, first, count)
            first += count
        stores = [
            Stored(results[k], targets[k], store_sems.at[k]) for k in range(len(outs))
        ]
        kernel(*operands, *stores, *refs[2:])
        for k in far:
            operands[k].wait()
        for store in stores:
            if not store.waited:
                store.wait()

    return pl.pallas_call(
        body,
        out_shape=[jax.ShapeDtypeStruct(s, t) for s, t in outs],
        in_specs=specs,
        out_specs=[HBM] * len(outs),
        scratch_shapes=held + [dma((max(sum(counts), 1),)), dma((len(outs),))] + list(scratch),
        compiler_params=pltpu.CompilerParams(vmem_limit_bytes=NEAR if near else ALL),
        cost_estimate=pl.CostEstimate(flops=flops, bytes_accessed=moved, transcendentals=0),
        name=name,
    )(*ins)


def exchange(x):
    return lax.all_to_all(x, AXES, split_axis=0, concat_axis=0, tiled=True)


def local(features, cotangent, w_self, w_neigh, bias, src_slot, dst_slot, edge_live, mirror_list):
    line = mirror_list.reshape(1, MIRRORS)
    lists = mirror_list[0].T
    square = ((1024, 1024), BF16)
    payload = ((PEERS, 16, F), BF16)

    (out1,) = call(pull_kernel, (lists, features), [((PEERS, 8, F), BF16)], "pull")
    got1 = exchange(out1)

    edges = (EDGES // LANES, LANES)
    rows_f32, rows_bf16 = ((1024, F), F32), ((1024, F), BF16)
    mm, mg, gm, gg, sums, tally = call(
        build_kernel,
        (edge_live, src_slot.reshape(edges), dst_slot.reshape(edges), features),
        [square] * 4 + [rows_f32, rows_bf16],
        "build",
        scalars=(0,),
        scratch=[
            pltpu.VMEM(edges, jnp.int32),
            pltpu.SMEM(edges, jnp.int32),
            pltpu.SemaphoreType.DMA,
        ]
        + [pltpu.VMEM((WORDS, 1, LANES), jnp.int32) for _ in range(COPIES)],
        flops=20_000_000_000,
        moved=20_000_000,
    )
    (out2,) = call(push_kernel, (got1, sums, gg, tally), [payload], "push", parts={2: PARTS})
    got2 = exchange(out2)
    gather, turned, sums_m, tally_m = call(
        local_kernel,
        (features, lists, mm, got1, mg),
        [square, ((F, MASTERS), BF16), rows_f32, rows_bf16],
        "local",
        flops=2_000_000_000,
        moved=6_000_000,
    )
    act, grad, msg, out3, total = call(
        dense_kernel,
        (
            line, got2, tally_m, sums_m, w_self, bias.reshape(1, H), features, w_neigh,
            cotangent, gather, turned,
        ),
        [((MASTERS, H), BF16), ((MASTERS, H), BF16), rows_bf16, payload, ((8, F), F32)],
        "dense",
    )
    got3 = exchange(out3)
    turned_gg, mirror, base = call(
        back_local_kernel,
        (gg, msg, mg, mm, grad, w_self, got2),
        [square, rows_f32, rows_f32],
        "back_local",
        idle=(6,),
        flops=2_000_000_000,
        moved=6_000_000,
    )
    (out4,) = call(
        back_push_kernel,
        (got3, mirror, total, turned_gg),
        [payload],
        "back_push",
        parts={3: PARTS},
    )
    got4 = exchange(out4)
    (base2,) = call(
        back_mirror_kernel,
        (got3, gm, base),
        [rows_f32],
        "back_mirror",
        flops=2_000_000_000,
        moved=6_000_000,
    )
    grad_features, grad_self, grad_neigh, bias_out = call(
        last_kernel,
        (line, got4, base2),
        [rows_bf16, ((F, H), F32), ((F, H), F32), ((2, F), F32)],
        "last",
        near=(1,),
    )
    return act, grad_features, grad_self, grad_neigh, bias_out.reshape(H)


def solution(mesh):
    placed = (
        P(AXES, None),
        P(AXES, None),
        P(),
        P(),
        P(),
        P(AXES),
        P(AXES),
        P(AXES),
        P(AXES, None, None),
    )
    return jax.shard_map(
        local,
        mesh=mesh,
        in_specs=placed,
        out_specs=(P(AXES, None), P(AXES, None), P(), P(), P()),
        check_vma=False,
    )
```

```python
import jax
import jax.numpy as jnp
from jax import lax
from jax.experimental import pallas as pl
from jax.experimental.pallas import tpu as pltpu
from jax.sharding import PartitionSpec as P

F32 = jnp.float32
BF16 = jnp.bfloat16
AXES = ("row", "col")

MASTERS = 1024
MIRRORS = 1024
SLOTS = MASTERS + MIRRORS
EDGES = 8192
PEERS = 128
F = 128
H = 256
LANES = 128
COPIES = 6
TURN = 256
PARTS = 4
WORDS = SLOTS * (SLOTS // 512)


def part_of(size, k):
    return pl.ds(k * (size // PARTS), size // PARTS)


def dot(a, b):
    return jnp.dot(a, b, preferred_element_type=F32)


def dot_nt(a, b):
    return lax.dot_general(a, b, (((1,), (1,)), ((), ())), preferred_element_type=F32)


def gather_matrix(column):
    places = lax.broadcasted_iota(jnp.int32, (MIRRORS, MASTERS), 1)
    return jnp.where(places == column, 1.0, 0.0).astype(BF16)


def scatter_matrix(line):
    places = lax.broadcasted_iota(jnp.int32, (MASTERS, MIRRORS), 0)
    return jnp.where(places == line, 1.0, 0.0).astype(BF16)


def diagonal(slots):
    shape = (PEERS, 8, 8)
    spread = jnp.broadcast_to(slots[:, None, :], shape)
    here = lax.broadcasted_iota(jnp.int32, shape, 1) == lax.broadcasted_iota(jnp.int32, shape, 2)
    return jnp.sum(jnp.where(here, spread, 0.0), axis=2, keepdims=True)


def as_column(lists):
    return diagonal(jnp.transpose(lists.astype(F32))).reshape(MIRRORS, 1).astype(jnp.int32)


def numbers():
    shape = (EDGES // LANES, LANES)
    row = lax.broadcasted_iota(jnp.int32, shape, 0) * LANES
    return row + lax.broadcasted_iota(jnp.int32, shape, 1)


def pull_kernel(
    live_ref, lists_ref, src_ref, dst_ref, rows_ref, out_ref, gather_ref, code_ref, hot_ref, low_ref
):
    gather_ref[...] = gather_matrix(as_column(lists_ref[...]))
    gather_ref.send()
    src, dst = src_ref[...], dst_ref[...]
    live = numbers() < live_ref[0]
    place = ((src >> 7) & 3) * SLOTS + dst
    code = place | ((src & 127) << 13) | ((src >> 9) << 24)
    code_ref[...] = jnp.where(live, code, 128 << 13)
    code_ref.send()
    slot = jnp.where(live, dst - MASTERS, -1)
    peer, low = slot >> 3, slot & 7
    peers = lax.broadcasted_iota(jnp.int32, (PEERS, LANES), 0)
    lows = lax.broadcasted_iota(jnp.int32, (16, LANES), 0)
    for k in range(EDGES // LANES):
        at = pl.ds(k * LANES, LANES)
        hot_ref[:, at] = jnp.where(peers == peer[k : k + 1], 1.0, 0.0).astype(BF16)
        low_ref[:, at] = jnp.where(lows == low[k : k + 1], 1.0, 0.0).astype(BF16)
    tally = jnp.broadcast_to(diagonal(dot_nt(hot_ref[...], low_ref[...])[:, :8]), (PEERS, 8, LANES))
    high, rest = split(tally)
    left = lax.broadcasted_iota(jnp.int32, tally.shape, 2) < LANES // 2
    tally = jnp.where(left, high, rest)
    rows = rows_ref[...]
    for c in range(2):
        picked = dot(gather_ref[c * 512 : (c + 1) * 512], rows).reshape(PEERS // 2, 8, F)
        half = pl.ds(c * (PEERS // 2), PEERS // 2)
        both = [picked, tally[c * (PEERS // 2) : (c + 1) * (PEERS // 2)]]
        out_ref[half] = jnp.concatenate(both, axis=1).astype(BF16)
        out_ref.send(half)


def build_kernel(
    live_ref, code_ref, rows_ref, mm_ref, mg_ref, gm_ref, gg_ref, sums_ref, codes, sem, *tables3
):
    load = pltpu.make_async_copy(code_ref, codes, sem)
    load.start()
    tables = [t.reshape(WORDS, LANES) for t in tables3]
    n = live_ref[0]

    def clear(i, carry):
        for t in tables:
            t[pl.ds(pl.multiple_of(i * 256, 256), 256), :] = jnp.zeros((256, LANES), jnp.int32)
        return carry

    lax.fori_loop(0, WORDS // 256, clear, 0)
    load.wait()

    lanes = lax.broadcasted_iota(jnp.int32, (1, LANES), 1) << 13
    one = jnp.ones((1, LANES), jnp.int32)

    def code_at(k, i):
        row, lane = divmod(k, LANES)
        part = codes.at[pl.ds(row, EDGES // LANES - TURN // LANES + 1), pl.ds(lane, 1)]
        return part[i * (TURN // LANES), 0]

    def turn(i, carry):
        for start in range(0, TURN, COPIES):
            count = min(COPIES, TURN - start)
            words = [code_at(start + k, i) for k in range(count)]
            where = [w & (WORDS - 1) for w in words]
            adds = []
            for w in words:
                w = jnp.full((1, LANES), w, jnp.int32)
                bit = lax.shift_left(one, lax.shift_right_logical(w, 21))
                adds.append(jnp.where(lanes == (w & (255 << 13)), bit, 0))
            olds = [tables3[k][where[k]] for k in range(count)]
            for k in range(count):
                tables3[k][where[k]] = olds[k] + adds[k]
        return carry

    turns = (n + TURN - 1) // TURN
    lax.fori_loop(0, turns, turn, 0)

    def put(near_ref, far_ref, to, at, read, seen):
        for j in range(4):
            words = read(pl.ds(pl.multiple_of(j * SLOTS + at, 128), 128))
            for q, counts in enumerate(words):
                half = near_ref if q < 2 else far_ref
                left = (q % 2) * 512 + j * LANES
                half[pl.ds(to, 128), pl.ds(left, LANES)] = counts.astype(F32).astype(BF16)
                seen = seen + jnp.sum(counts.reshape(16, 8, LANES), axis=0)
        return seen

    rows = rows_ref[...]

    def widen(read):
        def mirrors(i, seen):
            d = pl.multiple_of(i * 128, 128)
            return put(gm_ref, gg_ref, d, MASTERS + d, read, seen)

        def masters(i, seen):
            e = pl.multiple_of(i * 256, 256)
            sums_ref[pl.ds(e, 256), :] = dot(gm_ref[pl.ds(e, 256), :], rows)
            for h in range(2):
                d = pl.multiple_of(i * 256 + h * 128, 128)
                seen = put(mm_ref, mg_ref, d, d, read, seen)
            mm_ref.send(pl.ds(e, 256))
            mg_ref.send(pl.ds(e, 256))
            return seen

        seen = lax.fori_loop(0, MIRRORS // 128, mirrors, jnp.zeros((8, LANES), jnp.int32))
        gg_ref.send()
        gm_ref.send()
        seen = lax.fori_loop(0, MASTERS // 256, masters, seen)
        sums_ref.send()
        return seen

    def finish():
        for ref in (mm_ref, mg_ref, gm_ref, gg_ref, sums_ref):
            ref.wait()

    def read_bytes(at):
        x = tables[0][at, :]
        for t in tables[1:]:
            x = x + t[at, :]
        yield x & 255
        yield lax.shift_right_logical(x, 8) & 255
        yield lax.shift_right_logical(x, 16) & 255
        yield lax.shift_right_logical(x, 24)

    found = jnp.sum(widen(read_bytes).astype(F32))
    finish()

    @pl.when(found != n.astype(F32))
    def _():
        lax.fori_loop(0, WORDS // 256, clear, 0)

        def edge(e, carry):
            word = codes[e // LANES, e % LANES]
            at = word & (WORDS - 1)
            q = word >> 24
            one = jnp.where(
                lanes == (word & (127 << 13)), jnp.where(q % 2 == 1, 65536, 1), 0
            )
            tables3[0][at] = tables3[0][at] + jnp.where(q < 2, one, 0)
            tables3[1][at] = tables3[1][at] + jnp.where(q < 2, 0, one)
            return carry

        lax.fori_loop(0, n, edge, 0)

        def read_halves(at):
            for t in tables[:2]:
                x = t[at, :]
                yield x & 65535
                yield lax.shift_right_logical(x, 16)

        widen(read_halves)
        finish()


def split(x):
    high = x.astype(BF16).astype(F32)
    return high, (x - high).astype(BF16).astype(F32)


def parts_of(got):
    got = got.astype(F32)
    return got[:, :8].reshape(MIRRORS, F).astype(BF16), got[:, 8:]


def push_kernel(got_ref, sums_ref, gg_ref, out_ref):
    got, _ = parts_of(got_ref[...])
    for c in range(PARTS):
        rows, peers = part_of(MIRRORS, c), part_of(PEERS, c)
        sums = dot(gg_ref.part(c), got) + sums_ref[rows]
        out_ref[peers] = sums.reshape(PEERS // PARTS, 8, F).astype(BF16)
        out_ref.send(peers)


def local_kernel(
    got_ref, line_ref, rows_ref, mm_ref, mg_ref, turned_ref, sums_ref, inverse_ref
):
    both = got_ref[...].astype(F32)
    both = [both[:, :8].reshape(MIRRORS, F), both[:, 8:].reshape(MIRRORS, LANES)]
    both = jnp.concatenate(both, axis=1).astype(BF16)
    got, tally = both[:, :F], both[:, F:]
    degree = dot(scatter_matrix(line_ref[...]), tally)
    degree = degree + pltpu.roll(degree, LANES // 2, 1)
    rows = rows_ref[...]
    turned_ref[...] = rows.astype(F32).T.astype(BF16)
    turned_ref.send()
    ones = jnp.ones((MASTERS, LANES), BF16)
    both = dot(mm_ref[...], jnp.concatenate([rows, ones], axis=1)) + dot(
        mg_ref[...], jnp.concatenate([got, ones], axis=1)
    )
    sums_ref[...] = both[:, :F]
    sums_ref.send()
    inverse_ref[...] = 1.0 / jnp.maximum(both[:, F:] + degree, 1.0)
    inverse_ref.send()


def dense_kernel(
    got_ref, line_ref, sums_ref, inverse_ref, self_ref, bias_ref, rows_ref, neigh_ref, cot_ref,
    gather_ref, turned_ref,
    act_ref, grad_ref, msg_ref, out_ref, total_ref,
):
    got = got_ref[...].reshape(MIRRORS, F)
    w_self, w_neigh, bias, line = self_ref[...], neigh_ref[...], bias_ref[...], line_ref[...]
    size = MASTERS // PARTS
    terms, total = 0.0, 0.0
    for c in range(PARTS):
        rows = part_of(MASTERS, c)
        places = lax.broadcasted_iota(jnp.int32, (size, MIRRORS), 0) + c * size
        scatter = jnp.where(places == line, 1.0, 0.0).astype(BF16)
        inverse = inverse_ref[rows]
        mean = (sums_ref[rows] + dot(scatter, got)) * inverse
        pre = dot(rows_ref[rows], w_self) + dot(mean.astype(BF16), w_neigh) + bias
        sig = jax.nn.sigmoid(pre)
        act_ref[rows] = (pre * sig).astype(BF16)
        act_ref.send(rows)
        grad = (cot_ref[rows].astype(F32) * sig * (1.0 + pre * (1.0 - sig))).astype(BF16)
        grad_ref[rows] = grad
        grad_ref.send(rows)
        msg_ref[rows] = (dot_nt(grad, w_neigh) * inverse).astype(BF16)
        msg_ref.send(rows)
        turned = [turned_ref[:, c * size : (c + 1) * size], mean.T.astype(BF16)]
        terms = terms + dot(jnp.concatenate(turned, axis=0), grad)
        total = total + dot(jnp.ones((8, size), BF16), grad)
    flat = jnp.concatenate([terms[:, :F], terms[:, F:]], axis=0).reshape(PEERS // 2, 8, F)
    high, low = split(flat)
    first = lax.broadcasted_iota(jnp.int32, (PEERS // 2, 8, F), 1) < 4
    even = jnp.where(first, high, pltpu.roll(low, 4, 1))
    odd = jnp.where(first, pltpu.roll(high, 4, 1), low)
    mixed = jnp.stack([even, odd], axis=1).reshape(PEERS, 8, F)
    msg = msg_ref[...]
    for c in range(PARTS):
        peers, count = part_of(PEERS, c), PEERS // PARTS
        picked = dot(gather_ref.part(c), msg).reshape(count, 8, F)
        both = [picked, mixed[c * count : (c + 1) * count]]
        out_ref[peers] = jnp.concatenate(both, axis=1).astype(BF16)
        out_ref.send(peers)
    high, low = split(total)
    sub = lax.broadcasted_iota(jnp.int32, (8, F), 0)
    tile = jnp.where(sub == 4, high[:, :F], 0.0)
    tile = jnp.where(sub == 5, high[:, F:], tile)
    tile = jnp.where(sub == 6, low[:, :F], tile)
    total_ref[...] = jnp.where(sub == 7, low[:, F:], tile)
    total_ref.send()


def back_local_kernel(
    gg_ref, msg_ref, mg_ref, mm_ref, grad_ref, w_ref, turned_ref, mirror_ref, base_ref
):
    turned_ref[...] = gg_ref[...].T
    turned_ref.send()
    msg = msg_ref[...].astype(F32).T.astype(BF16)
    mirror_ref[...] = dot(msg, mg_ref[...]).T
    mirror_ref.send()
    base_ref[...] = dot(msg, mm_ref[...]).T + dot_nt(grad_ref[...], w_ref[...])
    base_ref.send()


def back_push_kernel(got_ref, mirror_ref, total_ref, turned_ref, out_ref):
    rows, terms = parts_of(got_ref[...])
    total = jnp.sum(terms, axis=0)
    total = total + pltpu.roll(total, 4, 0)
    sub = lax.broadcasted_iota(jnp.int32, (8, F), 0)
    tile = jnp.where(sub < 4, total, total_ref[...])
    shape = (PEERS // PARTS, 8, F)
    tiles = jnp.broadcast_to(tile[None], shape)
    for c in range(PARTS):
        peers = part_of(PEERS, c)
        spread = dot(turned_ref.part(c), rows) + mirror_ref[part_of(MIRRORS, c)]
        out_ref[peers] = jnp.concatenate([spread.reshape(shape), tiles], axis=1).astype(BF16)
        out_ref.send(peers)


def back_mirror_kernel(got_ref, gm_ref, base_ref, out_ref):
    turned = got_ref[...].astype(F32)[:, :8].reshape(MIRRORS, F).T.astype(BF16)
    out_ref[...] = dot(turned, gm_ref[...]).T + base_ref[...]
    out_ref.send()


def last_kernel(line_ref, got_ref, base_ref, grad_ref, self_ref, neigh_ref, bias_ref):
    rows, tiles = parts_of(got_ref[...])
    grad_ref[...] = (dot(scatter_matrix(line_ref[...]), rows) + base_ref[...]).astype(BF16)
    grad_ref.send()
    pairs = tiles.reshape(PEERS // 2, 2, 8, F)
    first = lax.broadcasted_iota(jnp.int32, (PEERS // 2, 8, F), 1) < 4
    flat = jnp.where(first, pairs[:, 0], pltpu.roll(pairs[:, 1], 4, 1)).reshape(2 * H, F)
    self_ref[:, :F] = flat[:F]
    self_ref[:, F:] = flat[H : H + F]
    neigh_ref[:, :F] = flat[F:H]
    neigh_ref[:, F:] = flat[H + F :]
    total = jnp.sum(tiles, axis=0)
    bias_ref[...] = total[4:6] + total[6:8]
    for ref in (self_ref, neigh_ref, bias_ref):
        ref.send()


VMEM = pl.BlockSpec(memory_space=pltpu.VMEM)
SMEM = pl.BlockSpec(memory_space=pltpu.SMEM)
HBM = pl.BlockSpec(memory_space=pltpu.HBM)
ALL = 60 * 1024 * 1024


class Loaded:
    def __init__(self, source, held, sems, first, parts):
        size = held.shape[0] // parts
        self.held, self.size = held, size
        self.copies = []
        for k in range(parts):
            rows = pl.ds(k * size, size)
            copy = pltpu.make_async_copy(source.at[rows], held.at[rows], sems.at[first + k])
            copy.start()
            self.copies.append(copy)

    def part(self, k):
        if self.copies[k] is not None:
            self.copies[k].wait()
            self.copies[k] = None
        return self.held[pl.ds(k * self.size, self.size)]

    def wait(self):
        for k, copy in enumerate(self.copies):
            if copy is not None:
                copy.wait()
                self.copies[k] = None

    def __getitem__(self, at):
        self.wait()
        return self.held[at]


class Stored:
    def __init__(self, held, target, sem):
        self.held, self.target, self.sem = held, target, sem
        self.copy = pltpu.make_async_copy(held, target, sem)
        self.waited = False

    def __setitem__(self, at, value):
        self.held[at] = value

    def __getitem__(self, at):
        return self.held[at]

    def wait(self):
        self.copy.wait()
        self.waited = True

    def send(self, rows=None):
        if rows is None:
            self.copy.start()
        else:
            pltpu.make_async_copy(self.held.at[rows], self.target.at[rows], self.sem).start()


def call(
    kernel, ins, outs, name, near=(), scalars=(), bare=(), scratch=(), parts=None,
    room=ALL, flops=0, moved=0,
):
    parts = parts or {}
    far = [k for k in range(len(ins)) if k not in (*near, *scalars, *bare)]
    specs = [VMEM if k in near else SMEM if k in scalars else HBM for k in range(len(ins))]
    held = [pltpu.VMEM(ins[k].shape, ins[k].dtype) for k in far]
    held += [pltpu.VMEM(s, t) for s, t in outs]
    counts = [parts.get(k, 1) for k in far]
    dma = pltpu.SemaphoreType.DMA

    def body(*refs):
        operands, refs = list(refs[: len(ins)]), refs[len(ins) :]
        results, refs = list(refs[: len(outs)]), refs[len(outs) :]
        copies, refs = refs[: len(far)], refs[len(far) :]
        holds, refs = refs[: len(outs)], refs[len(outs) :]
        load_sems, store_sems = refs[0], refs[1]
        first = 0
        for k, copy, count in zip(far, copies, counts, strict=True):
            operands[k] = Loaded(operands[k], copy, load_sems, first, count)
            first += count
        for k, hold in enumerate(holds):
            results[k] = Stored(hold, results[k], store_sems.at[k])
        kernel(*operands, *results, *refs[2:])
        for k in far:
            operands[k].wait()
        for result in results:
            if not result.waited:
                result.wait()

    return pl.pallas_call(
        body,
        out_shape=[jax.ShapeDtypeStruct(s, t) for s, t in outs],
        in_specs=specs,
        out_specs=[HBM] * len(outs),
        scratch_shapes=held + [dma((max(sum(counts), 1),)), dma((len(outs),))] + list(scratch),
        compiler_params=pltpu.CompilerParams(vmem_limit_bytes=room),
        cost_estimate=pl.CostEstimate(flops=flops, bytes_accessed=moved, transcendentals=0),
        name=name,
    )(*ins)


def exchange(x):
    return lax.all_to_all(x, AXES, split_axis=0, concat_axis=0, tiled=True)


def local(features, cotangent, w_self, w_neigh, bias, src_slot, dst_slot, edge_live, mirror_list):
    line = mirror_list.reshape(1, MIRRORS)
    lists = mirror_list[0].T
    square = ((1024, 1024), BF16)
    payload = ((PEERS, 16, F), BF16)

    edges = (EDGES // LANES, LANES)
    src, dst = src_slot.reshape(edges), dst_slot.reshape(edges)
    rows_f32, rows_bf16 = ((1024, F), F32), ((1024, F), BF16)
    out1, gather, code = call(
        pull_kernel,
        (edge_live, lists, src, dst, features),
        [payload, square, (edges, jnp.int32)],
        "pull",
        scalars=(0,),
        scratch=[pltpu.VMEM((PEERS, EDGES), BF16), pltpu.VMEM((16, EDGES), BF16)],
    )
    got1 = exchange(out1)
    mm, mg, gm, gg, sums = call(
        build_kernel,
        (edge_live, code, features),
        [square] * 4 + [rows_f32],
        "build",
        scalars=(0,),
        bare=(1,),
        scratch=[pltpu.SMEM(edges, jnp.int32), pltpu.SemaphoreType.DMA]
        + [pltpu.VMEM((WORDS, 1, LANES), jnp.int32) for _ in range(COPIES)],
        flops=20_000_000_000,
        moved=20_000_000,
    )
    (out2,) = call(
        push_kernel,
        (got1, sums, gg),
        [((PEERS, 8, F), BF16)],
        "push",
        near=(0,),
        room=55_400_000,
        parts={2: PARTS},
    )
    got2 = exchange(out2)
    turned, sums_m, inverse = call(
        local_kernel,
        (got1, line, features, mm, mg),
        [((F, MASTERS), BF16), rows_f32, rows_f32],
        "local",
        flops=2_000_000_000,
        moved=6_000_000,
    )
    act, grad, msg, out3, total = call(
        dense_kernel,
        (
            got2, line, sums_m, inverse, w_self, bias.reshape(1, H), features, w_neigh, cotangent,
            gather, turned,
        ),
        [((MASTERS, H), BF16), ((MASTERS, H), BF16), rows_bf16, payload, ((8, F), F32)],
        "dense",
        near=(0,),
        room=55_800_000,
        parts={9: PARTS},
    )
    got3 = exchange(out3)
    turned_gg, mirror, base = call(
        back_local_kernel,
        (gg, msg, mg, mm, grad, w_self),
        [square, rows_f32, rows_f32],
        "back_local",
        flops=2_000_000_000,
        moved=6_000_000,
    )
    (out4,) = call(
        back_push_kernel,
        (got3, mirror, total, turned_gg),
        [payload],
        "back_push",
        near=(0,),
        room=55_200_000,
        parts={3: PARTS},
    )
    got4 = exchange(out4)
    (base2,) = call(
        back_mirror_kernel,
        (got3, gm, base),
        [rows_f32],
        "back_mirror",
        flops=2_000_000_000,
        moved=6_000_000,
    )
    grad_features, grad_self, grad_neigh, bias_out = call(
        last_kernel,
        (line, got4, base2),
        [rows_bf16, ((F, H), F32), ((F, H), F32), ((2, F), F32)],
        "last",
        near=(1,),
        room=55_700_000,
    )
    return act, grad_features, grad_self, grad_neigh, bias_out.reshape(H)


def solution(mesh):
    placed = (
        P(AXES, None),
        P(AXES, None),
        P(),
        P(),
        P(),
        P(AXES),
        P(AXES),
        P(AXES),
        P(AXES, None, None),
    )
    return jax.shard_map(
        local,
        mesh=mesh,
        in_specs=placed,
        out_specs=(P(AXES, None), P(AXES, None), P(), P(), P()),
        check_vma=False,
    )
```

```python
import jax
import jax.numpy as jnp
from jax import lax
from jax.experimental import pallas as pl
from jax.experimental.pallas import tpu as pltpu
from jax.sharding import PartitionSpec as P

F32 = jnp.float32
BF16 = jnp.bfloat16
AXES = ("row", "col")

MASTERS = 1024
MIRRORS = 1024
SLOTS = MASTERS + MIRRORS
EDGES = 8192
PEERS = 128
F = 128
H = 256
LANES = 128
COPIES = 6
TURN = 256
PARTS = 4
WORDS = SLOTS * (SLOTS // 1024)


def part_of(size, k):
    return pl.ds(k * (size // PARTS), size // PARTS)


def dot(a, b):
    return jnp.dot(a, b, preferred_element_type=F32)


def dot_nt(a, b):
    return lax.dot_general(a, b, (((1,), (1,)), ((), ())), preferred_element_type=F32)


def gather_matrix(column):
    places = lax.broadcasted_iota(jnp.int32, (MIRRORS, MASTERS), 1)
    return jnp.where(places == column, 1.0, 0.0).astype(BF16)


def scatter_part(line, c):
    size = MASTERS // PARTS
    places = lax.broadcasted_iota(jnp.int32, (size, MIRRORS), 0) + c * size
    return jnp.where(places == line, 1.0, 0.0).astype(BF16)


def pick(slots, first):
    shape = (PEERS, 8, slots.shape[1])
    spread = jnp.broadcast_to(slots[:, None, :], shape)
    wanted = first + lax.broadcasted_iota(jnp.int32, shape, 1)
    here = lax.broadcasted_iota(jnp.int32, shape, 2) == wanted
    return jnp.sum(jnp.where(here, spread, 0.0), axis=2, keepdims=True)


def as_column(lists):
    return pick(jnp.transpose(lists.astype(F32)), 0).reshape(MIRRORS, 1).astype(jnp.int32)


def numbers():
    shape = (EDGES // LANES, LANES)
    row = lax.broadcasted_iota(jnp.int32, shape, 0) * LANES
    return row + lax.broadcasted_iota(jnp.int32, shape, 1)


def pull_kernel(
    live_ref, lists_ref, src_ref, dst_ref, rows_ref, out_ref, code_ref, high_ref, low_ref
):
    gather = gather_matrix(as_column(lists_ref[...]))
    src, dst = src_ref[...], dst_ref[...]
    live = numbers() < live_ref[0]
    place = ((src >> 7) & 1) * SLOTS + dst
    code = place | ((src & 127) << 12) | ((src >> 8) << 22)
    code_ref[...] = jnp.where(live, code, 128 << 12)
    code_ref.send()
    slot = jnp.where(live, dst - MASTERS, -1)
    high, low = slot >> 5, slot & 31
    places = lax.broadcasted_iota(jnp.int32, (32, LANES), 0)
    for k in range(EDGES // LANES):
        at = pl.ds(k * LANES, LANES)
        high_ref[:, at] = jnp.where(places == high[k : k + 1], 1.0, 0.0).astype(BF16)
        low_ref[:, at] = jnp.where(places == low[k : k + 1], 1.0, 0.0).astype(BF16)
    counts = dot_nt(high_ref[...], low_ref[...])
    peer = lax.broadcasted_iota(jnp.int32, (PEERS, 32), 0)
    of_peer = jnp.where(peer >> 2 == lax.broadcasted_iota(jnp.int32, (PEERS, 32), 1), 1.0, 0.0)
    counts = sum(dot(of_peer.astype(BF16), part.astype(BF16)) for part in split(counts))
    peer = lax.broadcasted_iota(jnp.int32, (PEERS, 8, 32), 0)
    tally = jnp.broadcast_to(pick(counts, (peer & 3) << 3), (PEERS, 8, LANES))
    high, rest = split(tally)
    left = lax.broadcasted_iota(jnp.int32, tally.shape, 2) < LANES // 2
    tally = jnp.where(left, high, rest)
    rows = rows_ref[...]
    for c in range(2):
        picked = dot(gather[c * 512 : (c + 1) * 512], rows).reshape(PEERS // 2, 8, F)
        half = pl.ds(c * (PEERS // 2), PEERS // 2)
        both = [picked, tally[c * (PEERS // 2) : (c + 1) * (PEERS // 2)]]
        out_ref[half] = jnp.concatenate(both, axis=1).astype(BF16)
        out_ref.send(half)


def build_kernel(
    live_ref, code_ref, rows_ref, mm_ref, mg_ref, gm_ref, gg_ref, sums_ref, codes, sem, *tables3
):
    load = pltpu.make_async_copy(code_ref, codes, sem)
    load.start()
    tables = [t.reshape(WORDS, LANES) for t in tables3]
    n = live_ref[0]

    def clear(i, carry):
        for t in tables:
            t[pl.ds(pl.multiple_of(i * 256, 256), 256), :] = jnp.zeros((256, LANES), jnp.int32)
        return carry

    lax.fori_loop(0, WORDS // 256, clear, 0)
    load.wait()

    lanes = lax.broadcasted_iota(jnp.int32, (1, LANES), 1) << 12
    one = jnp.ones((1, LANES), jnp.int32)

    def code_at(k, i):
        row, lane = divmod(k, LANES)
        part = codes.at[pl.ds(row, EDGES // LANES - TURN // LANES + 1), pl.ds(lane, 1)]
        return part[i * (TURN // LANES), 0]

    def turn(i, carry):
        for start in range(0, TURN, COPIES):
            count = min(COPIES, TURN - start)
            words = [code_at(start + k, i) for k in range(count)]
            where = [w & (WORDS - 1) for w in words]
            adds = []
            for w in words:
                w = jnp.full((1, LANES), w, jnp.int32)
                bit = lax.shift_left(one, lax.shift_right_logical(w, 20))
                adds.append(jnp.where(lanes == (w & (255 << 12)), bit, 0))
            olds = [tables3[k][where[k]] for k in range(count)]
            for k in range(count):
                tables3[k][where[k]] = olds[k] + adds[k]
        return carry

    turns = (n + TURN - 1) // TURN
    lax.fori_loop(0, turns, turn, 0)

    def put(near_ref, far_ref, to, at, read, seen):
        for j in range(2):
            words = read(pl.ds(pl.multiple_of(j * SLOTS + at, 128), 128))
            for q, counts in enumerate(words):
                half = near_ref if q < 4 else far_ref
                left = (q % 4) * 256 + j * LANES
                half[pl.ds(to, 128), pl.ds(left, LANES)] = counts.astype(F32).astype(BF16)
                seen = seen + jnp.sum(counts.reshape(16, 8, LANES), axis=0)
        return seen

    rows = rows_ref[...]

    def widen(read):
        def mirrors(i, seen):
            for h in range(2):
                d = pl.multiple_of(i * 256 + h * 128, 128)
                seen = put(gm_ref, gg_ref, d, MASTERS + d, read, seen)
            e = pl.multiple_of(i * 256, 256)
            gg_ref.send(pl.ds(e, 256))
            gm_ref.send(pl.ds(e, 256))
            return seen

        def masters(i, seen):
            e = pl.multiple_of(i * 256, 256)
            sums_ref[pl.ds(e, 256), :] = dot(gm_ref[pl.ds(e, 256), :], rows)
            for h in range(2):
                d = pl.multiple_of(i * 256 + h * 128, 128)
                seen = put(mm_ref, mg_ref, d, d, read, seen)
            mm_ref.send(pl.ds(e, 256))
            mg_ref.send(pl.ds(e, 256))
            return seen

        seen = lax.fori_loop(0, MIRRORS // 256, mirrors, jnp.zeros((8, LANES), jnp.int32))
        seen = lax.fori_loop(0, MASTERS // 256, masters, seen)
        sums_ref.send()
        return seen

    def finish():
        for ref in (mm_ref, mg_ref, gm_ref, gg_ref, sums_ref):
            ref.wait()

    def read_fours(at):
        x = tables[0][at, :]
        for t in tables[1:]:
            x = x + t[at, :]
        yield x & 15
        for q in range(1, 7):
            yield lax.shift_right_logical(x, 4 * q) & 15
        yield lax.shift_right_logical(x, 28)

    found = jnp.sum(widen(read_fours).astype(F32))
    finish()

    @pl.when(found != n.astype(F32))
    def _():
        lax.fori_loop(0, WORDS // 256, clear, 0)

        def edge(e, carry):
            word = codes[e // LANES, e % LANES]
            at = word & (WORDS - 1)
            q = word >> 22
            one = jnp.where(lanes == (word & (127 << 12)), jnp.where(q >= 4, 65536, 1), 0)
            for k in range(4):
                tables3[k][at] = tables3[k][at] + jnp.where(q % 4 == k, one, 0)
            return carry

        lax.fori_loop(0, n, edge, 0)

        def read_halves(at):
            for t in tables[:4]:
                yield t[at, :] & 65535
            for t in tables[:4]:
                yield lax.shift_right_logical(t[at, :], 16)

        widen(read_halves)
        finish()


def split(x):
    high = x.astype(BF16).astype(F32)
    return high, (x - high).astype(BF16).astype(F32)


def parts_of(got):
    got = got.astype(F32)
    return got[:, :8].reshape(MIRRORS, F).astype(BF16), got[:, 8:]


def two_parts(x):
    high, low = split(x)
    left = lax.broadcasted_iota(jnp.int32, x.shape, 1) < LANES // 2
    return jnp.where(left, high, low).astype(BF16)


def push_kernel(got_ref, sums_ref, gg_ref, out_ref):
    got, _ = parts_of(got_ref[...])
    for c in range(PARTS):
        rows, peers = part_of(MIRRORS, c), part_of(PEERS, c)
        sums = dot(gg_ref.part(c), got) + sums_ref[rows]
        out_ref[peers] = sums.reshape(PEERS // PARTS, 8, F).astype(BF16)
        out_ref.send(peers)


def local_kernel(
    got_ref, rows_ref, mg_ref, mm_ref, turned_ref, told_ref, sums_ref, tally_ref
):
    rows = rows_ref[...]
    turned_ref[...] = rows.astype(F32).T.astype(BF16)
    turned_ref.send()
    both = got_ref[...].astype(F32)
    both = [both[:, :8].reshape(MIRRORS, F), both[:, 8:].reshape(MIRRORS, LANES)]
    both = jnp.concatenate(both, axis=1).astype(BF16)
    told_ref[...] = both[:, F:]
    told_ref.send()
    ones = jnp.ones((MASTERS, LANES), BF16)
    near = jnp.concatenate([rows, ones], axis=1)
    far = jnp.concatenate([both[:, :F], ones], axis=1)
    for c in range(PARTS):
        part = part_of(MASTERS, c)
        both = dot(mg_ref.part(c), far) + dot(mm_ref.part(c), near)
        sums_ref[part] = both[:, :F]
        sums_ref.send(part)
        tally_ref[part] = two_parts(both[:, F:])
        tally_ref.send(part)


def dense_kernel(
    got_ref, line_ref, told_ref, tally_ref, sums_ref, rows_ref, self_ref, neigh_ref, bias_ref,
    cot_ref, turned_ref,
    act_ref, own_ref, msg_ref, out_ref, total_ref,
):
    line = line_ref[...]
    wide = jnp.concatenate([got_ref[...].reshape(MIRRORS, F), told_ref[...]], axis=1)
    w = jnp.concatenate([self_ref[...], neigh_ref[...]], axis=0)
    bias = bias_ref[...]
    size = MASTERS // PARTS
    terms, total, picked = 0.0, 0.0, 0.0
    for c in range(PARTS):
        rows = part_of(MASTERS, c)
        scatter = scatter_part(line, c)
        folded = dot(scatter, wide)
        degree = folded[:, F:] + tally_ref[rows].astype(F32)
        degree = degree + pltpu.roll(degree, LANES // 2, 1)
        inverse = 1.0 / jnp.maximum(degree, 1.0)
        mean = (sums_ref[rows] + folded[:, :F]) * inverse
        pre = dot(jnp.concatenate([rows_ref[rows], mean.astype(BF16)], axis=1), w) + bias
        sig = jax.nn.sigmoid(pre)
        act_ref[rows] = (pre * sig).astype(BF16)
        act_ref.send(rows)
        grad = (cot_ref[rows].astype(F32) * sig * (1.0 + pre * (1.0 - sig))).astype(BF16)
        back = dot_nt(grad, w)
        own_ref[rows] = back[:, :F]
        own_ref.send(rows)
        msg = back[:, F:] * inverse
        msg_ref[rows] = msg.astype(BF16)
        msg_ref.send(rows)
        picked = picked + dot(msg.T.astype(BF16), scatter)
        turned = [turned_ref[:, c * size : (c + 1) * size], mean.T.astype(BF16)]
        terms = terms + dot(jnp.concatenate(turned, axis=0), grad)
        total = total + dot(jnp.ones((8, size), BF16), grad)
    flat = jnp.concatenate([terms[:, :F], terms[:, F:]], axis=0).reshape(PEERS // 2, 8, F)
    high, low = split(flat)
    first = lax.broadcasted_iota(jnp.int32, (PEERS // 2, 8, F), 1) < 4
    even = jnp.where(first, high, pltpu.roll(low, 4, 1))
    odd = jnp.where(first, pltpu.roll(high, 4, 1), low)
    mixed = jnp.stack([even, odd], axis=1).reshape(PEERS, 8, F)
    for c in range(PARTS):
        peers, count = part_of(PEERS, c), PEERS // PARTS
        rows = picked[:, c * 8 * count : (c + 1) * 8 * count].T.reshape(count, 8, F)
        both = [rows, mixed[c * count : (c + 1) * count]]
        out_ref[peers] = jnp.concatenate(both, axis=1).astype(BF16)
        out_ref.send(peers)
    high, low = split(total)
    sub = lax.broadcasted_iota(jnp.int32, (8, F), 0)
    tile = jnp.where(sub == 4, high[:, :F], 0.0)
    tile = jnp.where(sub == 5, high[:, F:], tile)
    tile = jnp.where(sub == 6, low[:, :F], tile)
    total_ref[...] = jnp.where(sub == 7, low[:, F:], tile)
    total_ref.send()


def back_local_kernel(
    gg_ref, msg_ref, mg_ref, mm_ref, own_ref, turned_ref, mirror_ref, base_ref
):
    turned_ref[...] = gg_ref[...].T
    turned_ref.send()
    msg = msg_ref[...].astype(F32).T.astype(BF16)
    mirror_ref[...] = dot(msg, mg_ref[...]).T
    mirror_ref.send()
    base_ref[...] = dot(msg, mm_ref[...]).T + own_ref[...]
    base_ref.send()


def back_push_kernel(got_ref, mirror_ref, total_ref, turned_ref, out_ref):
    rows, terms = parts_of(got_ref[...])
    total = jnp.sum(terms, axis=0)
    total = total + pltpu.roll(total, 4, 0)
    sub = lax.broadcasted_iota(jnp.int32, (8, F), 0)
    tile = jnp.where(sub < 4, total, total_ref[...])
    shape = (PEERS // PARTS, 8, F)
    tiles = jnp.broadcast_to(tile[None], shape)
    for c in range(PARTS):
        peers = part_of(PEERS, c)
        spread = dot(turned_ref.part(c), rows) + mirror_ref[part_of(MIRRORS, c)]
        out_ref[peers] = jnp.concatenate([spread.reshape(shape), tiles], axis=1).astype(BF16)
        out_ref.send(peers)


def back_mirror_kernel(got_ref, gm_ref, base_ref, out_ref):
    turned = got_ref[...].astype(F32)[:, :8].reshape(MIRRORS, F).T.astype(BF16)
    out_ref[...] = dot(turned, gm_ref[...]).T + base_ref[...]
    out_ref.send()


def last_kernel(line_ref, got_ref, base_ref, grad_ref, self_ref, neigh_ref, bias_ref):
    rows, tiles = parts_of(got_ref[...])
    line = line_ref[...]
    for c in range(PARTS):
        part = part_of(MASTERS, c)
        grad_ref[part] = (dot(scatter_part(line, c), rows) + base_ref[part]).astype(BF16)
        grad_ref.send(part)
    pairs = tiles.reshape(PEERS // 2, 2, 8, F)
    first = lax.broadcasted_iota(jnp.int32, (PEERS // 2, 8, F), 1) < 4
    flat = jnp.where(first, pairs[:, 0], pltpu.roll(pairs[:, 1], 4, 1)).reshape(2 * H, F)
    self_ref[:, :F] = flat[:F]
    self_ref[:, F:] = flat[H : H + F]
    neigh_ref[:, :F] = flat[F:H]
    neigh_ref[:, F:] = flat[H + F :]
    total = jnp.sum(tiles, axis=0)
    bias_ref[...] = total[4:6] + total[6:8]
    for ref in (self_ref, neigh_ref, bias_ref):
        ref.send()


VMEM = pl.BlockSpec(memory_space=pltpu.VMEM)
SMEM = pl.BlockSpec(memory_space=pltpu.SMEM)
HBM = pl.BlockSpec(memory_space=pltpu.HBM)
ALL = 60 * 1024 * 1024


class Loaded:
    def __init__(self, source, held, sems, first, parts):
        size = held.shape[0] // parts
        self.held, self.size = held, size
        self.copies = []
        for k in range(parts):
            rows = pl.ds(k * size, size)
            copy = pltpu.make_async_copy(source.at[rows], held.at[rows], sems.at[first + k])
            copy.start()
            self.copies.append(copy)

    def part(self, k):
        if self.copies[k] is not None:
            self.copies[k].wait()
            self.copies[k] = None
        return self.held[pl.ds(k * self.size, self.size)]

    def wait(self):
        for k, copy in enumerate(self.copies):
            if copy is not None:
                copy.wait()
                self.copies[k] = None

    def __getitem__(self, at):
        self.wait()
        return self.held[at]


class Stored:
    def __init__(self, held, target, sem):
        self.held, self.target, self.sem = held, target, sem
        self.copy = pltpu.make_async_copy(held, target, sem)
        self.waited = False

    def __setitem__(self, at, value):
        self.held[at] = value

    def __getitem__(self, at):
        return self.held[at]

    def wait(self):
        self.copy.wait()
        self.waited = True

    def send(self, rows=None):
        if rows is None:
            self.copy.start()
        else:
            pltpu.make_async_copy(self.held.at[rows], self.target.at[rows], self.sem).start()


def call(
    kernel, ins, outs, name, near=(), scalars=(), bare=(), scratch=(), parts=None,
    room=ALL, flops=0, moved=0,
):
    parts = parts or {}
    far = [k for k in range(len(ins)) if k not in (*near, *scalars, *bare)]
    specs = [VMEM if k in near else SMEM if k in scalars else HBM for k in range(len(ins))]
    held = [pltpu.VMEM(ins[k].shape, ins[k].dtype) for k in far]
    held += [pltpu.VMEM(s, t) for s, t in outs]
    counts = [parts.get(k, 1) for k in far]
    dma = pltpu.SemaphoreType.DMA

    def body(*refs):
        operands, refs = list(refs[: len(ins)]), refs[len(ins) :]
        results, refs = list(refs[: len(outs)]), refs[len(outs) :]
        copies, refs = refs[: len(far)], refs[len(far) :]
        holds, refs = refs[: len(outs)], refs[len(outs) :]
        load_sems, store_sems = refs[0], refs[1]
        first = 0
        for k, copy, count in zip(far, copies, counts, strict=True):
            operands[k] = Loaded(operands[k], copy, load_sems, first, count)
            first += count
        for k, hold in enumerate(holds):
            results[k] = Stored(hold, results[k], store_sems.at[k])
        kernel(*operands, *results, *refs[2:])
        for k in far:
            operands[k].wait()
        for result in results:
            if not result.waited:
                result.wait()

    return pl.pallas_call(
        body,
        out_shape=[jax.ShapeDtypeStruct(s, t) for s, t in outs],
        in_specs=specs,
        out_specs=[HBM] * len(outs),
        scratch_shapes=held + [dma((max(sum(counts), 1),)), dma((len(outs),))] + list(scratch),
        compiler_params=pltpu.CompilerParams(vmem_limit_bytes=room),
        cost_estimate=pl.CostEstimate(flops=flops, bytes_accessed=moved, transcendentals=0),
        name=name,
    )(*ins)


def exchange(x):
    return lax.all_to_all(x, AXES, split_axis=0, concat_axis=0, tiled=True)


def local(features, cotangent, w_self, w_neigh, bias, src_slot, dst_slot, edge_live, mirror_list):
    line = mirror_list.reshape(1, MIRRORS)
    lists = mirror_list[0].T
    square = ((1024, 1024), BF16)
    payload = ((PEERS, 16, F), BF16)

    edges = (EDGES // LANES, LANES)
    src, dst = src_slot.reshape(edges), dst_slot.reshape(edges)
    rows_f32, rows_bf16 = ((1024, F), F32), ((1024, F), BF16)
    out1, code = call(
        pull_kernel,
        (edge_live, lists, src, dst, features),
        [payload, (edges, jnp.int32)],
        "pull",
        scalars=(0,),
        scratch=[pltpu.VMEM((32, EDGES), BF16), pltpu.VMEM((32, EDGES), BF16)],
    )
    got1 = exchange(out1)
    mm, mg, gm, gg, sums = call(
        build_kernel,
        (edge_live, code, features),
        [square] * 4 + [rows_f32],
        "build",
        scalars=(0,),
        bare=(1,),
        scratch=[pltpu.SMEM(edges, jnp.int32), pltpu.SemaphoreType.DMA]
        + [pltpu.VMEM((WORDS, 1, LANES), jnp.int32) for _ in range(COPIES)],
        flops=20_000_000_000,
        moved=20_000_000,
    )
    (out2,) = call(
        push_kernel,
        (got1, sums, gg),
        [((PEERS, 8, F), BF16)],
        "push",
        near=(0,),
        room=55_400_000,
        parts={2: PARTS},
    )
    got2 = exchange(out2)
    turned, told, sums_m, tally = call(
        local_kernel,
        (got1, features, mg, mm),
        [((F, MASTERS), BF16), rows_bf16, rows_f32, rows_bf16],
        "local",
        parts={2: PARTS, 3: PARTS},
        flops=2_000_000_000,
        moved=6_000_000,
    )
    act, own, msg, out3, total = call(
        dense_kernel,
        (
            got2, line, told, tally, sums_m, features, w_self, w_neigh, bias.reshape(1, H),
            cotangent, turned,
        ),
        [((MASTERS, H), BF16), rows_f32, rows_bf16, payload, ((8, F), F32)],
        "dense",
        near=(0,),
        room=55_800_000,
    )
    got3 = exchange(out3)
    turned_gg, mirror, base = call(
        back_local_kernel,
        (gg, msg, mg, mm, own),
        [square, rows_f32, rows_f32],
        "back_local",
        flops=2_000_000_000,
        moved=6_000_000,
    )
    (out4,) = call(
        back_push_kernel,
        (got3, mirror, total, turned_gg),
        [payload],
        "back_push",
        near=(0,),
        room=55_200_000,
        parts={3: PARTS},
    )
    got4 = exchange(out4)
    (base2,) = call(
        back_mirror_kernel,
        (got3, gm, base),
        [rows_f32],
        "back_mirror",
        flops=2_000_000_000,
        moved=6_000_000,
    )
    grad_features, grad_self, grad_neigh, bias_out = call(
        last_kernel,
        (line, got4, base2),
        [rows_bf16, ((F, H), F32), ((F, H), F32), ((2, F), F32)],
        "last",
        near=(1,),
        room=55_700_000,
    )
    return act, grad_features, grad_self, grad_neigh, bias_out.reshape(H)


def solution(mesh):
    placed = (
        P(AXES, None),
        P(AXES, None),
        P(),
        P(),
        P(),
        P(AXES),
        P(AXES),
        P(AXES),
        P(AXES, None, None),
    )
    return jax.shard_map(
        local,
        mesh=mesh,
        in_specs=placed,
        out_specs=(P(AXES, None), P(AXES, None), P(), P(), P()),
        check_vma=False,
    )
```

```python
import jax
import jax.numpy as jnp
from jax import lax
from jax.experimental import pallas as pl
from jax.experimental.pallas import tpu as pltpu
from jax.sharding import PartitionSpec as P

F32 = jnp.float32
BF16 = jnp.bfloat16
AXES = ("row", "col")

MASTERS = 1024
MIRRORS = 1024
SLOTS = MASTERS + MIRRORS
EDGES = 8192
PEERS = 128
F = 128
H = 256
LANES = 128
COPIES = 6
TURN = 256
PARTS = 4
WORDS = SLOTS * (SLOTS // 1024)


def part_of(size, k, parts=PARTS):
    return pl.ds(k * (size // parts), size // parts)


def dot(a, b):
    return jnp.dot(a, b, preferred_element_type=F32)


def dot_nt(a, b):
    return lax.dot_general(a, b, (((1,), (1,)), ((), ())), preferred_element_type=F32)


def gather_matrix(column):
    places = lax.broadcasted_iota(jnp.int32, (MIRRORS, MASTERS), 1)
    return jnp.where(places == column, 1.0, 0.0).astype(BF16)


def scatter_part(line, c, parts=PARTS):
    size = MASTERS // parts
    places = lax.broadcasted_iota(jnp.int32, (size, MIRRORS), 0) + c * size
    return jnp.where(places == line, 1.0, 0.0).astype(BF16)


def pick(slots, first):
    shape = (PEERS, 8, slots.shape[1])
    spread = jnp.broadcast_to(slots[:, None, :], shape)
    wanted = first + lax.broadcasted_iota(jnp.int32, shape, 1)
    here = lax.broadcasted_iota(jnp.int32, shape, 2) == wanted
    return jnp.sum(jnp.where(here, spread, 0.0), axis=2, keepdims=True)


def as_column(lists):
    return pick(jnp.transpose(lists.astype(F32)), 0).reshape(MIRRORS, 1).astype(jnp.int32)


def numbers():
    shape = (EDGES // LANES, LANES)
    row = lax.broadcasted_iota(jnp.int32, shape, 0) * LANES
    return row + lax.broadcasted_iota(jnp.int32, shape, 1)


def pull_kernel(
    live_ref, lists_ref, src_ref, dst_ref, rows_ref, out_ref, code_ref, high_ref, low_ref
):
    gather = gather_matrix(as_column(lists_ref[...]))
    src, dst = src_ref[...], dst_ref[...]
    live = numbers() < live_ref[0]
    place = ((src >> 7) & 1) * SLOTS + dst
    code = place | ((src & 127) << 12) | ((src >> 8) << 22)
    code_ref[...] = jnp.where(live, code, 128 << 12)
    code_ref.send()
    slot = jnp.where(live, dst - MASTERS, -1)
    high, low = slot >> 5, slot & 31
    places = lax.broadcasted_iota(jnp.int32, (32, LANES), 0)
    for k in range(EDGES // LANES):
        at = pl.ds(k * LANES, LANES)
        high_ref[:, at] = jnp.where(places == high[k : k + 1], 1.0, 0.0).astype(BF16)
        low_ref[:, at] = jnp.where(places == low[k : k + 1], 1.0, 0.0).astype(BF16)
    counts = dot_nt(high_ref[...], low_ref[...])
    peer = lax.broadcasted_iota(jnp.int32, (PEERS, 32), 0)
    of_peer = jnp.where(peer >> 2 == lax.broadcasted_iota(jnp.int32, (PEERS, 32), 1), 1.0, 0.0)
    counts = sum(dot(of_peer.astype(BF16), part.astype(BF16)) for part in split(counts))
    peer = lax.broadcasted_iota(jnp.int32, (PEERS, 8, 32), 0)
    tally = jnp.broadcast_to(pick(counts, (peer & 3) << 3), (PEERS, 8, LANES))
    high, rest = split(tally)
    left = lax.broadcasted_iota(jnp.int32, tally.shape, 2) < LANES // 2
    tally = jnp.where(left, high, rest)
    rows = rows_ref[...]
    for c in range(2):
        picked = dot(gather[c * 512 : (c + 1) * 512], rows).reshape(PEERS // 2, 8, F)
        half = pl.ds(c * (PEERS // 2), PEERS // 2)
        both = [picked, tally[c * (PEERS // 2) : (c + 1) * (PEERS // 2)]]
        out_ref[half] = jnp.concatenate(both, axis=1).astype(BF16)
        out_ref.send(half)


def build_kernel(
    live_ref, code_ref, rows_ref, mm_ref, mg_ref, gm_ref, gg_ref, sums_ref, codes, sem, *tables3
):
    load = pltpu.make_async_copy(code_ref, codes, sem)
    load.start()
    tables = [t.reshape(WORDS, LANES) for t in tables3]
    n = live_ref[0]

    def clear(i, carry):
        for t in tables:
            t[pl.ds(pl.multiple_of(i * 256, 256), 256), :] = jnp.zeros((256, LANES), jnp.int32)
        return carry

    lax.fori_loop(0, WORDS // 256, clear, 0)
    load.wait()

    lanes = lax.broadcasted_iota(jnp.int32, (1, LANES), 1) << 12
    one = jnp.ones((1, LANES), jnp.int32)

    def code_at(k, i):
        row, lane = divmod(k, LANES)
        part = codes.at[pl.ds(row, EDGES // LANES - TURN // LANES + 1), pl.ds(lane, 1)]
        return part[i * (TURN // LANES), 0]

    def turn(i, carry):
        for start in range(0, TURN, COPIES):
            count = min(COPIES, TURN - start)
            words = [code_at(start + k, i) for k in range(count)]
            where = [w & (WORDS - 1) for w in words]
            adds = []
            for w in words:
                w = jnp.full((1, LANES), w, jnp.int32)
                bit = lax.shift_left(one, lax.shift_right_logical(w, 20))
                adds.append(jnp.where(lanes == (w & (255 << 12)), bit, 0))
            olds = [tables3[k][where[k]] for k in range(count)]
            for k in range(count):
                tables3[k][where[k]] = olds[k] + adds[k]
        return carry

    turns = (n + TURN - 1) // TURN
    lax.fori_loop(0, turns, turn, 0)

    def put(near_ref, far_ref, to, at, read, seen):
        for j in range(2):
            words = read(pl.ds(pl.multiple_of(j * SLOTS + at, 128), 128))
            for q, counts in enumerate(words):
                half = near_ref if q < 4 else far_ref
                left = (q % 4) * 256 + j * LANES
                half[pl.ds(to, 128), pl.ds(left, LANES)] = counts.astype(F32).astype(BF16)
                seen = seen + jnp.sum(counts.reshape(16, 8, LANES), axis=0)
        return seen

    rows = rows_ref[...]

    def widen(read):
        def mirrors(i, seen):
            for h in range(2):
                d = pl.multiple_of(i * 256 + h * 128, 128)
                seen = put(gm_ref, gg_ref, d, MASTERS + d, read, seen)
            e = pl.multiple_of(i * 256, 256)
            gg_ref.send(pl.ds(e, 256))
            gm_ref.send(pl.ds(e, 256))
            return seen

        def masters(i, seen):
            e = pl.multiple_of(i * 256, 256)
            sums_ref[pl.ds(e, 256), :] = dot(gm_ref[pl.ds(e, 256), :], rows)
            for h in range(2):
                d = pl.multiple_of(i * 256 + h * 128, 128)
                seen = put(mm_ref, mg_ref, d, d, read, seen)
            mm_ref.send(pl.ds(e, 256))
            mg_ref.send(pl.ds(e, 256))
            return seen

        seen = lax.fori_loop(0, MIRRORS // 256, mirrors, jnp.zeros((8, LANES), jnp.int32))
        seen = lax.fori_loop(0, MASTERS // 256, masters, seen)
        sums_ref.send()
        return seen

    def finish():
        for ref in (mm_ref, mg_ref, gm_ref, gg_ref, sums_ref):
            ref.wait()

    def read_fours(at):
        x = tables[0][at, :]
        for t in tables[1:]:
            x = x + t[at, :]
        yield x & 15
        for q in range(1, 7):
            yield lax.shift_right_logical(x, 4 * q) & 15
        yield lax.shift_right_logical(x, 28)

    found = jnp.sum(widen(read_fours).astype(F32))
    finish()

    @pl.when(found != n.astype(F32))
    def _():
        lax.fori_loop(0, WORDS // 256, clear, 0)

        def edge(e, carry):
            word = codes[e // LANES, e % LANES]
            at = word & (WORDS - 1)
            q = word >> 22
            one = jnp.where(lanes == (word & (127 << 12)), jnp.where(q >= 4, 65536, 1), 0)
            for k in range(4):
                tables3[k][at] = tables3[k][at] + jnp.where(q % 4 == k, one, 0)
            return carry

        lax.fori_loop(0, n, edge, 0)

        def read_halves(at):
            for t in tables[:4]:
                yield t[at, :] & 65535
            for t in tables[:4]:
                yield lax.shift_right_logical(t[at, :], 16)

        widen(read_halves)
        finish()


def split(x):
    high = x.astype(BF16).astype(F32)
    return high, (x - high).astype(BF16).astype(F32)


def parts_of(got):
    got = got.astype(F32)
    return got[:, :8].reshape(MIRRORS, F).astype(BF16), got[:, 8:]


def two_parts(x):
    high, low = split(x)
    left = lax.broadcasted_iota(jnp.int32, x.shape, 1) < LANES // 2
    return jnp.where(left, high, low).astype(BF16)


def push_kernel(got_ref, sums_ref, gg_ref, out_ref):
    got, _ = parts_of(got_ref[...])
    for c in range(PARTS):
        rows, peers = part_of(MIRRORS, c), part_of(PEERS, c)
        sums = dot(gg_ref.part(c), got) + sums_ref[rows]
        out_ref[peers] = sums.reshape(PEERS // PARTS, 8, F).astype(BF16)
        out_ref.send(peers)


def local_kernel(
    got_ref, rows_ref, mg_ref, mm_ref, turned_ref, told_ref, sums_ref, tally_ref
):
    rows = rows_ref[...]
    turned_ref[...] = rows.astype(F32).T.astype(BF16)
    turned_ref.send()
    both = got_ref[...].astype(F32)
    both = [both[:, :8].reshape(MIRRORS, F), both[:, 8:].reshape(MIRRORS, LANES)]
    both = jnp.concatenate(both, axis=1).astype(BF16)
    told_ref[...] = both[:, F:]
    told_ref.send()
    ones = jnp.ones((MASTERS, LANES), BF16)
    near = jnp.concatenate([rows, ones], axis=1)
    far = jnp.concatenate([both[:, :F], ones], axis=1)
    both = dot(mg_ref[...], far) + dot(mm_ref[...], near)
    sums_ref[...] = both[:, :F]
    sums_ref.send()
    tally_ref[...] = two_parts(both[:, F:])
    tally_ref.send()


def dense_kernel(
    got_ref, line_ref, told_ref, tally_ref, sums_ref, rows_ref, self_ref, neigh_ref, bias_ref,
    cot_ref, turned_ref,
    act_ref, own_ref, msg_ref, out_ref, total_ref,
):
    line = line_ref[...]
    wide = jnp.concatenate([got_ref[...].reshape(MIRRORS, F), told_ref[...]], axis=1)
    w = jnp.concatenate([self_ref[...], neigh_ref[...]], axis=0)
    bias = bias_ref[...]
    size = MASTERS // 2
    scatters = [scatter_part(line, c, 2) for c in range(2)]
    folds = [dot(scatter, wide) for scatter in scatters]
    terms, total, picked = 0.0, 0.0, 0.0
    for c in range(2):
        rows, scatter, folded = part_of(MASTERS, c, 2), scatters[c], folds[c]
        degree = folded[:, F:] + tally_ref[rows].astype(F32)
        degree = degree + pltpu.roll(degree, LANES // 2, 1)
        inverse = 1.0 / jnp.maximum(degree, 1.0)
        mean = (sums_ref[rows] + folded[:, :F]) * inverse
        pre = dot(jnp.concatenate([rows_ref[rows], mean.astype(BF16)], axis=1), w) + bias
        sig = jax.nn.sigmoid(pre)
        act_ref[rows] = (pre * sig).astype(BF16)
        grad = (cot_ref[rows].astype(F32) * sig * (1.0 + pre * (1.0 - sig))).astype(BF16)
        back = dot_nt(grad, w)
        own_ref[rows] = back[:, :F]
        msg = back[:, F:] * inverse
        msg_ref[rows] = msg.astype(BF16)
        for ref in (act_ref, own_ref, msg_ref):
            ref.send(rows)
        picked = picked + dot(msg.T.astype(BF16), scatter)
        turned = [turned_ref[:, c * size : (c + 1) * size], mean.T.astype(BF16)]
        terms = terms + dot(jnp.concatenate(turned, axis=0), grad)
        total = total + dot(jnp.ones((8, size), BF16), grad)
    flat = jnp.concatenate([terms[:, :F], terms[:, F:]], axis=0).reshape(PEERS // 2, 8, F)
    high, low = split(flat)
    first = lax.broadcasted_iota(jnp.int32, (PEERS // 2, 8, F), 1) < 4
    even = jnp.where(first, high, pltpu.roll(low, 4, 1))
    odd = jnp.where(first, pltpu.roll(high, 4, 1), low)
    mixed = jnp.stack([even, odd], axis=1).reshape(PEERS, 8, F)
    for c in range(2):
        peers, count = part_of(PEERS, c, 2), PEERS // 2
        rows = picked[:, c * 8 * count : (c + 1) * 8 * count].T.reshape(count, 8, F)
        both = [rows, mixed[c * count : (c + 1) * count]]
        out_ref[peers] = jnp.concatenate(both, axis=1).astype(BF16)
        out_ref.send(peers)
    high, low = split(total)
    sub = lax.broadcasted_iota(jnp.int32, (8, F), 0)
    tile = jnp.where(sub == 4, high[:, :F], 0.0)
    tile = jnp.where(sub == 5, high[:, F:], tile)
    tile = jnp.where(sub == 6, low[:, :F], tile)
    total_ref[...] = jnp.where(sub == 7, low[:, F:], tile)
    total_ref.send()


def back_local_kernel(
    gg_ref, msg_ref, mg_ref, mm_ref, own_ref, turned_ref, mirror_ref, base_ref
):
    turned_ref[...] = gg_ref[...].T
    turned_ref.send()
    msg = msg_ref[...].astype(F32).T.astype(BF16)
    mirror_ref[...] = dot(msg, mg_ref[...]).T
    mirror_ref.send()
    base_ref[...] = dot(msg, mm_ref[...]).T + own_ref[...]
    base_ref.send()


def back_push_kernel(got_ref, mirror_ref, total_ref, turned_ref, out_ref):
    rows, terms = parts_of(got_ref[...])
    total = jnp.sum(terms, axis=0)
    total = total + pltpu.roll(total, 4, 0)
    sub = lax.broadcasted_iota(jnp.int32, (8, F), 0)
    tile = jnp.where(sub < 4, total, total_ref[...])
    shape = (PEERS // PARTS, 8, F)
    tiles = jnp.broadcast_to(tile[None], shape)
    for c in range(PARTS):
        peers = part_of(PEERS, c)
        spread = dot(turned_ref.part(c), rows) + mirror_ref[part_of(MIRRORS, c)]
        out_ref[peers] = jnp.concatenate([spread.reshape(shape), tiles], axis=1).astype(BF16)
        out_ref.send(peers)


def back_mirror_kernel(got_ref, gm_ref, base_ref, out_ref):
    turned = got_ref[...].astype(F32)[:, :8].reshape(MIRRORS, F).T.astype(BF16)
    out_ref[...] = dot(turned, gm_ref[...]).T + base_ref[...]
    out_ref.send()


def last_kernel(line_ref, got_ref, base_ref, grad_ref, self_ref, neigh_ref, bias_ref):
    rows, tiles = parts_of(got_ref[...])
    line = line_ref[...]
    for c in range(PARTS):
        part = part_of(MASTERS, c)
        grad_ref[part] = (dot(scatter_part(line, c), rows) + base_ref[part]).astype(BF16)
        grad_ref.send(part)
    pairs = tiles.reshape(PEERS // 2, 2, 8, F)
    first = lax.broadcasted_iota(jnp.int32, (PEERS // 2, 8, F), 1) < 4
    flat = jnp.where(first, pairs[:, 0], pltpu.roll(pairs[:, 1], 4, 1)).reshape(2 * H, F)
    self_ref[:, :F] = flat[:F]
    self_ref[:, F:] = flat[H : H + F]
    neigh_ref[:, :F] = flat[F:H]
    neigh_ref[:, F:] = flat[H + F :]
    total = jnp.sum(tiles, axis=0)
    bias_ref[...] = total[4:6] + total[6:8]
    for ref in (self_ref, neigh_ref, bias_ref):
        ref.send()


VMEM = pl.BlockSpec(memory_space=pltpu.VMEM)
SMEM = pl.BlockSpec(memory_space=pltpu.SMEM)
HBM = pl.BlockSpec(memory_space=pltpu.HBM)
ALL = 60 * 1024 * 1024


class Loaded:
    def __init__(self, source, held, sems, first, parts):
        size = held.shape[0] // parts
        self.held, self.size = held, size
        self.copies = []
        for k in range(parts):
            rows = pl.ds(k * size, size)
            copy = pltpu.make_async_copy(source.at[rows], held.at[rows], sems.at[first + k])
            copy.start()
            self.copies.append(copy)

    def part(self, k):
        if self.copies[k] is not None:
            self.copies[k].wait()
            self.copies[k] = None
        return self.held[pl.ds(k * self.size, self.size)]

    def wait(self):
        for k, copy in enumerate(self.copies):
            if copy is not None:
                copy.wait()
                self.copies[k] = None

    def __getitem__(self, at):
        self.wait()
        return self.held[at]


class Stored:
    def __init__(self, held, target, sem):
        self.held, self.target, self.sem = held, target, sem
        self.copy = pltpu.make_async_copy(held, target, sem)
        self.waited = False

    def __setitem__(self, at, value):
        self.held[at] = value

    def __getitem__(self, at):
        return self.held[at]

    def wait(self):
        self.copy.wait()
        self.waited = True

    def send(self, rows=None):
        if rows is None:
            self.copy.start()
        else:
            pltpu.make_async_copy(self.held.at[rows], self.target.at[rows], self.sem).start()


def call(
    kernel, ins, outs, name, near=(), scalars=(), bare=(), scratch=(), parts=None,
    room=ALL, flops=0, moved=0,
):
    parts = parts or {}
    far = [k for k in range(len(ins)) if k not in (*near, *scalars, *bare)]
    specs = [VMEM if k in near else SMEM if k in scalars else HBM for k in range(len(ins))]
    held = [pltpu.VMEM(ins[k].shape, ins[k].dtype) for k in far]
    held += [pltpu.VMEM(s, t) for s, t in outs]
    counts = [parts.get(k, 1) for k in far]
    dma = pltpu.SemaphoreType.DMA

    def body(*refs):
        operands, refs = list(refs[: len(ins)]), refs[len(ins) :]
        results, refs = list(refs[: len(outs)]), refs[len(outs) :]
        copies, refs = refs[: len(far)], refs[len(far) :]
        holds, refs = refs[: len(outs)], refs[len(outs) :]
        load_sems, store_sems = refs[0], refs[1]
        first = 0
        for k, copy, count in zip(far, copies, counts, strict=True):
            operands[k] = Loaded(operands[k], copy, load_sems, first, count)
            first += count
        for k, hold in enumerate(holds):
            results[k] = Stored(hold, results[k], store_sems.at[k])
        kernel(*operands, *results, *refs[2:])
        for k in far:
            operands[k].wait()
        for result in results:
            if not result.waited:
                result.wait()

    return pl.pallas_call(
        body,
        out_shape=[jax.ShapeDtypeStruct(s, t) for s, t in outs],
        in_specs=specs,
        out_specs=[HBM] * len(outs),
        scratch_shapes=held + [dma((max(sum(counts), 1),)), dma((len(outs),))] + list(scratch),
        compiler_params=pltpu.CompilerParams(vmem_limit_bytes=room),
        cost_estimate=pl.CostEstimate(flops=flops, bytes_accessed=moved, transcendentals=0),
        name=name,
    )(*ins)


def exchange(x):
    return lax.all_to_all(x, AXES, split_axis=0, concat_axis=0, tiled=True)


def local(features, cotangent, w_self, w_neigh, bias, src_slot, dst_slot, edge_live, mirror_list):
    line = mirror_list.reshape(1, MIRRORS)
    lists = mirror_list[0].T
    square = ((1024, 1024), BF16)
    payload = ((PEERS, 16, F), BF16)

    edges = (EDGES // LANES, LANES)
    src, dst = src_slot.reshape(edges), dst_slot.reshape(edges)
    rows_f32, rows_bf16 = ((1024, F), F32), ((1024, F), BF16)
    out1, code = call(
        pull_kernel,
        (edge_live, lists, src, dst, features),
        [payload, (edges, jnp.int32)],
        "pull",
        scalars=(0,),
        scratch=[pltpu.VMEM((32, EDGES), BF16), pltpu.VMEM((32, EDGES), BF16)],
    )
    got1 = exchange(out1)
    mm, mg, gm, gg, sums = call(
        build_kernel,
        (edge_live, code, features),
        [square] * 4 + [rows_f32],
        "build",
        scalars=(0,),
        bare=(1,),
        scratch=[pltpu.SMEM(edges, jnp.int32), pltpu.SemaphoreType.DMA]
        + [pltpu.VMEM((WORDS, 1, LANES), jnp.int32) for _ in range(COPIES)],
        flops=20_000_000_000,
        moved=20_000_000,
    )
    (out2,) = call(
        push_kernel,
        (got1, sums, gg),
        [((PEERS, 8, F), BF16)],
        "push",
        near=(0,),
        room=55_400_000,
        parts={2: PARTS},
    )
    got2 = exchange(out2)
    turned, told, sums_m, tally = call(
        local_kernel,
        (got1, features, mg, mm),
        [((F, MASTERS), BF16), rows_bf16, rows_f32, rows_bf16],
        "local",
        flops=2_000_000_000,
        moved=6_000_000,
    )
    act, own, msg, out3, total = call(
        dense_kernel,
        (
            got2, line, told, tally, sums_m, features, w_self, w_neigh, bias.reshape(1, H),
            cotangent, turned,
        ),
        [((MASTERS, H), BF16), rows_f32, rows_bf16, payload, ((8, F), F32)],
        "dense",
        near=(0,),
        room=55_800_000,
    )
    got3 = exchange(out3)
    turned_gg, mirror, base = call(
        back_local_kernel,
        (gg, msg, mg, mm, own),
        [square, rows_f32, rows_f32],
        "back_local",
        flops=2_000_000_000,
        moved=6_000_000,
    )
    (out4,) = call(
        back_push_kernel,
        (got3, mirror, total, turned_gg),
        [payload],
        "back_push",
        near=(0,),
        room=55_200_000,
        parts={3: PARTS},
    )
    got4 = exchange(out4)
    (base2,) = call(
        back_mirror_kernel,
        (got3, gm, base),
        [rows_f32],
        "back_mirror",
        flops=2_000_000_000,
        moved=6_000_000,
    )
    grad_features, grad_self, grad_neigh, bias_out = call(
        last_kernel,
        (line, got4, base2),
        [rows_bf16, ((F, H), F32), ((F, H), F32), ((2, F), F32)],
        "last",
        near=(1,),
        room=55_700_000,
    )
    return act, grad_features, grad_self, grad_neigh, bias_out.reshape(H)


def solution(mesh):
    placed = (
        P(AXES, None),
        P(AXES, None),
        P(),
        P(),
        P(),
        P(AXES),
        P(AXES),
        P(AXES),
        P(AXES, None, None),
    )
    return jax.shard_map(
        local,
        mesh=mesh,
        in_specs=placed,
        out_specs=(P(AXES, None), P(AXES, None), P(), P(), P()),
        check_vma=False,
    )
```

```python
import jax
import jax.numpy as jnp
from jax import lax
from jax.experimental import pallas as pl
from jax.experimental.pallas import tpu as pltpu
from jax.sharding import PartitionSpec as P

F32 = jnp.float32
BF16 = jnp.bfloat16
AXES = ("row", "col")

MASTERS = 1024
MIRRORS = 1024
SLOTS = MASTERS + MIRRORS
EDGES = 8192
PEERS = 128
F = 128
H = 256
LANES = 128
COPIES = 6
TURN = 256
PARTS = 4
WORDS = SLOTS * (SLOTS // 1024)


def part_of(size, k, parts=PARTS):
    return pl.ds(k * (size // parts), size // parts)


def dot(a, b):
    return jnp.dot(a, b, preferred_element_type=F32)


def dot_nt(a, b):
    return lax.dot_general(a, b, (((1,), (1,)), ((), ())), preferred_element_type=F32)


def gather_matrix(column):
    places = lax.broadcasted_iota(jnp.int32, (MIRRORS, MASTERS), 1)
    return jnp.where(places == column, 1.0, 0.0).astype(BF16)


def scatter_part(line, c, parts=PARTS):
    size = MASTERS // parts
    places = lax.broadcasted_iota(jnp.int32, (size, MIRRORS), 0) + c * size
    return jnp.where(places == line, 1.0, 0.0).astype(BF16)


def pick(slots, first):
    shape = (PEERS, 8, slots.shape[1])
    spread = jnp.broadcast_to(slots[:, None, :], shape)
    wanted = first + lax.broadcasted_iota(jnp.int32, shape, 1)
    here = lax.broadcasted_iota(jnp.int32, shape, 2) == wanted
    return jnp.sum(jnp.where(here, spread, 0.0), axis=2, keepdims=True)


def as_column(lists):
    return pick(jnp.transpose(lists.astype(F32)), 0).reshape(MIRRORS, 1).astype(jnp.int32)


def numbers():
    shape = (EDGES // LANES, LANES)
    row = lax.broadcasted_iota(jnp.int32, shape, 0) * LANES
    return row + lax.broadcasted_iota(jnp.int32, shape, 1)


def pull_kernel(
    live_ref, lists_ref, src_ref, dst_ref, rows_ref, out_ref, code_ref, high_ref, low_ref
):
    gather = gather_matrix(as_column(lists_ref[...]))
    src, dst = src_ref[...], dst_ref[...]
    live = numbers() < live_ref[0]
    place = ((src >> 7) & 1) * SLOTS + dst
    code = place | ((src & 127) << 12) | ((src >> 8) << 22)
    code_ref[...] = jnp.where(live, code, 128 << 12)
    code_ref.send()
    slot = jnp.where(live, dst - MASTERS, -1)
    high, low = slot >> 5, slot & 31
    places = lax.broadcasted_iota(jnp.int32, (32, LANES), 0)
    for k in range(EDGES // LANES):
        at = pl.ds(k * LANES, LANES)
        high_ref[:, at] = jnp.where(places == high[k : k + 1], 1.0, 0.0).astype(BF16)
        low_ref[:, at] = jnp.where(places == low[k : k + 1], 1.0, 0.0).astype(BF16)
    counts = dot_nt(high_ref[...], low_ref[...])
    peer = lax.broadcasted_iota(jnp.int32, (PEERS, 32), 0)
    of_peer = jnp.where(peer >> 2 == lax.broadcasted_iota(jnp.int32, (PEERS, 32), 1), 1.0, 0.0)
    counts = sum(dot(of_peer.astype(BF16), part.astype(BF16)) for part in split(counts))
    peer = lax.broadcasted_iota(jnp.int32, (PEERS, 8, 32), 0)
    tally = jnp.broadcast_to(pick(counts, (peer & 3) << 3), (PEERS, 8, LANES))
    high, rest = split(tally)
    left = lax.broadcasted_iota(jnp.int32, tally.shape, 2) < LANES // 2
    tally = jnp.where(left, high, rest)
    rows = rows_ref[...]
    for c in range(2):
        picked = dot(gather[c * 512 : (c + 1) * 512], rows).reshape(PEERS // 2, 8, F)
        half = pl.ds(c * (PEERS // 2), PEERS // 2)
        both = [picked, tally[c * (PEERS // 2) : (c + 1) * (PEERS // 2)]]
        out_ref[half] = jnp.concatenate(both, axis=1).astype(BF16)
        out_ref.send(half)


def fours(x):
    yield x & 15
    for q in range(1, 7):
        yield lax.shift_right_logical(x, 4 * q) & 15
    yield lax.shift_right_logical(x, 28)


def put(near_ref, far_ref, row, j, counts):
    for q, count in enumerate(counts):
        half = near_ref if q < 4 else far_ref
        left = (q % 4) * 256 + j * LANES
        half[pl.ds(row, 128), pl.ds(left, LANES)] = count.astype(F32).astype(BF16)


def load_masters(flag_ref, words_ref, mm_hbm, mg_hbm, mm, mg, sem):
    words_ref.wait()

    @pl.when(flag_ref[0] == 0)
    def _():
        def block(i, carry):
            d = pl.multiple_of(i * 128, 128)
            for j in range(2):
                at = pl.ds(pl.multiple_of(j * MASTERS + d, 128), 128)
                put(mm, mg, d, j, fours(words_ref[at, :]))
            return carry

        lax.fori_loop(0, MASTERS // 128, block, 0)

    @pl.when(flag_ref[0] != 0)
    def _():
        for source, target in ((mm_hbm, mm), (mg_hbm, mg)):
            copy = pltpu.make_async_copy(source, target, sem)
            copy.start()
            copy.wait()


def build_kernel(
    live_ref, code_ref, rows_ref, words_ref, gm_ref, gg_ref, sums_ref, flag_ref, mm_hbm, mg_hbm,
    codes, sem, mm, mg, *tables3
):
    load = pltpu.make_async_copy(code_ref, codes, sem)
    load.start()
    tables = [t.reshape(WORDS, LANES) for t in tables3]
    n = live_ref[0]

    def clear(i, carry):
        for t in tables:
            t[pl.ds(pl.multiple_of(i * 256, 256), 256), :] = jnp.zeros((256, LANES), jnp.int32)
        return carry

    lax.fori_loop(0, WORDS // 256, clear, 0)
    load.wait()

    lanes = lax.broadcasted_iota(jnp.int32, (1, LANES), 1) << 12
    one = jnp.ones((1, LANES), jnp.int32)

    def code_at(k, i):
        row, lane = divmod(k, LANES)
        part = codes.at[pl.ds(row, EDGES // LANES - TURN // LANES + 1), pl.ds(lane, 1)]
        return part[i * (TURN // LANES), 0]

    def turn(i, carry):
        for start in range(0, TURN, COPIES):
            count = min(COPIES, TURN - start)
            words = [code_at(start + k, i) for k in range(count)]
            where = [w & (WORDS - 1) for w in words]
            adds = []
            for w in words:
                w = jnp.full((1, LANES), w, jnp.int32)
                bit = lax.shift_left(one, lax.shift_right_logical(w, 20))
                adds.append(jnp.where(lanes == (w & (255 << 12)), bit, 0))
            olds = [tables3[k][where[k]] for k in range(count)]
            for k in range(count):
                tables3[k][where[k]] = olds[k] + adds[k]
        return carry

    turns = (n + TURN - 1) // TURN
    lax.fori_loop(0, turns, turn, 0)

    rows = rows_ref[...]
    none = jnp.zeros((8, LANES), jnp.int32)

    def add_up(x):
        return jnp.sum(x.reshape(16, 8, LANES), axis=0)

    def table_sum(j, row):
        at = pl.ds(pl.multiple_of(j * SLOTS + row, 128), 128)
        x = tables[0][at, :]
        for t in tables[1:]:
            x = x + t[at, :]
        return x

    def mirrors(i, seen):
        e = pl.multiple_of(i * 256, 256)
        for h in range(2):
            d = pl.multiple_of(i * 256 + h * 128, 128)
            for j in range(2):
                counts = list(fours(table_sum(j, MASTERS + d)))
                put(gm_ref, gg_ref, d, j, counts)
                for count in counts:
                    seen = seen + add_up(count)
        gg_ref.send(pl.ds(e, 256))
        gm_ref.send(pl.ds(e, 256))
        return seen

    def masters(i, seen):
        e = pl.multiple_of(i * 256, 256)
        sums_ref[pl.ds(e, 256), :] = dot(gm_ref[pl.ds(e, 256), :], rows)
        for j in range(2):
            for h in range(2):
                x = table_sum(j, pl.multiple_of(i * 256 + h * 128, 128))
                words_ref[pl.ds(pl.multiple_of(j * MASTERS + e + h * 128, 128), 128), :] = x
                pairs = (x & 0x0F0F0F0F) + (lax.shift_right_logical(x, 4) & 0x0F0F0F0F)
                fourth = (pairs & 0x00FF00FF) + (lax.shift_right_logical(pairs, 8) & 0x00FF00FF)
                seen = seen + add_up(fourth)
            words_ref.send(pl.ds(pl.multiple_of(j * MASTERS + e, 256), 256))
        return seen

    def finish():
        sums_ref.send()
        for ref in (words_ref, gm_ref, gg_ref, sums_ref):
            ref.wait()

    seen = lax.fori_loop(0, MIRRORS // 256, mirrors, none)
    halves = lax.fori_loop(0, MASTERS // 256, masters, none)
    seen = seen + (halves & 0xFFFF) + lax.shift_right_logical(halves, 16)
    found = jnp.sum(seen.astype(F32))
    finish()
    flag_ref[0] = jnp.where(found != n.astype(F32), 1, 0)

    @pl.when(found != n.astype(F32))
    def _():
        lax.fori_loop(0, WORDS // 256, clear, 0)

        def edge(e, carry):
            word = codes[e // LANES, e % LANES]
            at = word & (WORDS - 1)
            q = word >> 22
            one = jnp.where(lanes == (word & (127 << 12)), jnp.where(q >= 4, 65536, 1), 0)
            for k in range(4):
                tables3[k][at] = tables3[k][at] + jnp.where(q % 4 == k, one, 0)
            return carry

        lax.fori_loop(0, n, edge, 0)

        def wide(j, row):
            at = pl.ds(pl.multiple_of(j * SLOTS + row, 128), 128)
            found = [t[at, :] for t in tables[:4]]
            return [x & 65535 for x in found] + [lax.shift_right_logical(x, 16) for x in found]

        def block(i, carry):
            d = pl.multiple_of(i * 128, 128)
            for j in range(2):
                put(gm_ref, gg_ref, d, j, wide(j, MASTERS + d))
                put(mm, mg, d, j, wide(j, d))
            sums_ref[pl.ds(d, 128), :] = dot(gm_ref[pl.ds(d, 128), :], rows)
            return carry

        lax.fori_loop(0, MASTERS // 128, block, 0)
        words_ref.send()
        gm_ref.send()
        gg_ref.send()
        finish()
        for source, target in ((mm, mm_hbm), (mg, mg_hbm)):
            copy = pltpu.make_async_copy(source, target, sem)
            copy.start()
            copy.wait()


def split(x):
    high = x.astype(BF16).astype(F32)
    return high, (x - high).astype(BF16).astype(F32)


def parts_of(got):
    got = got.astype(F32)
    return got[:, :8].reshape(MIRRORS, F).astype(BF16), got[:, 8:]


def two_parts(x):
    high, low = split(x)
    left = lax.broadcasted_iota(jnp.int32, x.shape, 1) < LANES // 2
    return jnp.where(left, high, low).astype(BF16)


def push_kernel(got_ref, sums_ref, gg_ref, out_ref):
    got, _ = parts_of(got_ref[...])
    for c in range(PARTS):
        rows, peers = part_of(MIRRORS, c), part_of(PEERS, c)
        sums = dot(gg_ref.part(c), got) + sums_ref[rows]
        out_ref[peers] = sums.reshape(PEERS // PARTS, 8, F).astype(BF16)
        out_ref.send(peers)


def local_kernel(
    flag_ref, got_ref, rows_ref, words_ref, mm_hbm, mg_hbm,
    turned_ref, told_ref, sums_ref, tally_ref, mm, mg, sem,
):
    rows = rows_ref[...]
    turned_ref[...] = rows.astype(F32).T.astype(BF16)
    turned_ref.send()
    both = got_ref[...].astype(F32)
    both = [both[:, :8].reshape(MIRRORS, F), both[:, 8:].reshape(MIRRORS, LANES)]
    both = jnp.concatenate(both, axis=1).astype(BF16)
    told_ref[...] = both[:, F:]
    told_ref.send()
    ones = jnp.ones((MASTERS, LANES), BF16)
    near = jnp.concatenate([rows, ones], axis=1)
    far = jnp.concatenate([both[:, :F], ones], axis=1)
    load_masters(flag_ref, words_ref, mm_hbm, mg_hbm, mm, mg, sem)
    both = dot(mg[...], far) + dot(mm[...], near)
    sums_ref[...] = both[:, :F]
    sums_ref.send()
    tally_ref[...] = two_parts(both[:, F:])
    tally_ref.send()


def dense_kernel(
    got_ref, line_ref, told_ref, tally_ref, sums_ref, rows_ref, self_ref, neigh_ref, bias_ref,
    cot_ref, turned_ref,
    act_ref, own_ref, msg_ref, out_ref, total_ref,
):
    line = line_ref[...]
    wide = jnp.concatenate([got_ref[...].reshape(MIRRORS, F), told_ref[...]], axis=1)
    w = jnp.concatenate([self_ref[...], neigh_ref[...]], axis=0)
    bias = bias_ref[...]
    size = MASTERS // 2
    scatters = [scatter_part(line, c, 2) for c in range(2)]
    folds = [dot(scatter, wide) for scatter in scatters]
    terms, total, picked = 0.0, 0.0, 0.0
    for c in range(2):
        rows, scatter, folded = part_of(MASTERS, c, 2), scatters[c], folds[c]
        degree = folded[:, F:] + tally_ref[rows].astype(F32)
        degree = degree + pltpu.roll(degree, LANES // 2, 1)
        inverse = 1.0 / jnp.maximum(degree, 1.0)
        mean = (sums_ref[rows] + folded[:, :F]) * inverse
        pre = dot(jnp.concatenate([rows_ref[rows], mean.astype(BF16)], axis=1), w) + bias
        sig = jax.nn.sigmoid(pre)
        act_ref[rows] = (pre * sig).astype(BF16)
        grad = (cot_ref[rows].astype(F32) * sig * (1.0 + pre * (1.0 - sig))).astype(BF16)
        back = dot_nt(grad, w)
        own_ref[rows] = back[:, :F]
        msg = back[:, F:] * inverse
        msg_ref[rows] = msg
        for ref in (act_ref, own_ref, msg_ref):
            ref.send(rows)
        picked = picked + dot(msg.T.astype(BF16), scatter)
        turned = [turned_ref[:, c * size : (c + 1) * size], mean.T.astype(BF16)]
        terms = terms + dot(jnp.concatenate(turned, axis=0), grad)
        total = total + dot(jnp.ones((8, size), BF16), grad)
    flat = jnp.concatenate([terms[:, :F], terms[:, F:]], axis=0).reshape(PEERS // 2, 8, F)
    high, low = split(flat)
    first = lax.broadcasted_iota(jnp.int32, (PEERS // 2, 8, F), 1) < 4
    even = jnp.where(first, high, pltpu.roll(low, 4, 1))
    odd = jnp.where(first, pltpu.roll(high, 4, 1), low)
    mixed = jnp.stack([even, odd], axis=1).reshape(PEERS, 8, F)
    for c in range(2):
        peers, count = part_of(PEERS, c, 2), PEERS // 2
        rows = picked[:, c * 8 * count : (c + 1) * 8 * count].T.reshape(count, 8, F)
        both = [rows, mixed[c * count : (c + 1) * count]]
        out_ref[peers] = jnp.concatenate(both, axis=1).astype(BF16)
        out_ref.send(peers)
    high, low = split(total)
    sub = lax.broadcasted_iota(jnp.int32, (8, F), 0)
    tile = jnp.where(sub == 4, high[:, :F], 0.0)
    tile = jnp.where(sub == 5, high[:, F:], tile)
    tile = jnp.where(sub == 6, low[:, :F], tile)
    total_ref[...] = jnp.where(sub == 7, low[:, F:], tile)
    total_ref.send()


def back_local_kernel(
    flag_ref, gg_ref, msg_ref, words_ref, own_ref, mm_hbm, mg_hbm,
    turned_ref, mirror_ref, base_ref, mm, mg, sem,
):
    turned_ref[...] = gg_ref[...].T
    turned_ref.send()
    msg = msg_ref[...].T.astype(BF16)
    load_masters(flag_ref, words_ref, mm_hbm, mg_hbm, mm, mg, sem)
    mirror_ref[...] = dot(msg, mg[...]).T
    mirror_ref.send()
    base_ref[...] = dot(msg, mm[...]).T + own_ref[...]
    base_ref.send()


def back_push_kernel(got_ref, mirror_ref, total_ref, turned_ref, out_ref):
    rows, terms = parts_of(got_ref[...])
    total = jnp.sum(terms, axis=0)
    total = total + pltpu.roll(total, 4, 0)
    sub = lax.broadcasted_iota(jnp.int32, (8, F), 0)
    tile = jnp.where(sub < 4, total, total_ref[...])
    shape = (PEERS // PARTS, 8, F)
    tiles = jnp.broadcast_to(tile[None], shape)
    for c in range(PARTS):
        peers = part_of(PEERS, c)
        spread = dot(turned_ref.part(c), rows) + mirror_ref[part_of(MIRRORS, c)]
        out_ref[peers] = jnp.concatenate([spread.reshape(shape), tiles], axis=1).astype(BF16)
        out_ref.send(peers)


def back_mirror_kernel(got_ref, gm_ref, base_ref, out_ref):
    turned = got_ref[...].astype(F32)[:, :8].reshape(MIRRORS, F).T.astype(BF16)
    out_ref[...] = dot(turned, gm_ref[...]).T + base_ref[...]
    out_ref.send()


def last_kernel(line_ref, got_ref, base_ref, grad_ref, self_ref, neigh_ref, bias_ref):
    rows, tiles = parts_of(got_ref[...])
    line = line_ref[...]
    for c in range(PARTS):
        part = part_of(MASTERS, c)
        grad_ref[part] = (dot(scatter_part(line, c), rows) + base_ref[part]).astype(BF16)
        grad_ref.send(part)
    pairs = tiles.reshape(PEERS // 2, 2, 8, F)
    first = lax.broadcasted_iota(jnp.int32, (PEERS // 2, 8, F), 1) < 4
    flat = jnp.where(first, pairs[:, 0], pltpu.roll(pairs[:, 1], 4, 1)).reshape(2 * H, F)
    self_ref[:, :F] = flat[:F]
    self_ref[:, F:] = flat[H : H + F]
    neigh_ref[:, :F] = flat[F:H]
    neigh_ref[:, F:] = flat[H + F :]
    total = jnp.sum(tiles, axis=0)
    bias_ref[...] = total[4:6] + total[6:8]
    for ref in (self_ref, neigh_ref, bias_ref):
        ref.send()


VMEM = pl.BlockSpec(memory_space=pltpu.VMEM)
SMEM = pl.BlockSpec(memory_space=pltpu.SMEM)
HBM = pl.BlockSpec(memory_space=pltpu.HBM)
ALL = 60 * 1024 * 1024


class Loaded:
    def __init__(self, source, held, sems, first, parts):
        size = held.shape[0] // parts
        self.held, self.size = held, size
        self.copies = []
        for k in range(parts):
            rows = pl.ds(k * size, size)
            copy = pltpu.make_async_copy(source.at[rows], held.at[rows], sems.at[first + k])
            copy.start()
            self.copies.append(copy)

    def part(self, k):
        if self.copies[k] is not None:
            self.copies[k].wait()
            self.copies[k] = None
        return self.held[pl.ds(k * self.size, self.size)]

    def wait(self):
        for k, copy in enumerate(self.copies):
            if copy is not None:
                copy.wait()
                self.copies[k] = None

    def __getitem__(self, at):
        self.wait()
        return self.held[at]


class Stored:
    def __init__(self, held, target, sem):
        self.held, self.target, self.sem = held, target, sem
        self.copy = pltpu.make_async_copy(held, target, sem)
        self.waited = False

    def __setitem__(self, at, value):
        self.held[at] = value

    def __getitem__(self, at):
        return self.held[at]

    def wait(self):
        self.copy.wait()
        self.waited = True

    def send(self, rows=None):
        if rows is None:
            self.copy.start()
        else:
            pltpu.make_async_copy(self.held.at[rows], self.target.at[rows], self.sem).start()


def call(
    kernel, ins, outs, name, near=(), scalars=(), bare=(), plain=None, scratch=(), parts=None,
    room=ALL, flops=0, moved=0,
):
    parts, plain = parts or {}, plain or {}
    away = [k for k in range(len(outs)) if k not in plain]
    far = [k for k in range(len(ins)) if k not in (*near, *scalars, *bare)]
    specs = [VMEM if k in near else SMEM if k in scalars else HBM for k in range(len(ins))]
    held = [pltpu.VMEM(ins[k].shape, ins[k].dtype) for k in far]
    held += [pltpu.VMEM(*outs[k]) for k in away]
    counts = [parts.get(k, 1) for k in far]
    dma = pltpu.SemaphoreType.DMA

    def body(*refs):
        operands, refs = list(refs[: len(ins)]), refs[len(ins) :]
        results, refs = list(refs[: len(outs)]), refs[len(outs) :]
        copies, refs = refs[: len(far)], refs[len(far) :]
        holds, refs = refs[: len(away)], refs[len(away) :]
        load_sems, store_sems = refs[0], refs[1]
        first = 0
        for k, copy, count in zip(far, copies, counts, strict=True):
            operands[k] = Loaded(operands[k], copy, load_sems, first, count)
            first += count
        for n, (k, hold) in enumerate(zip(away, holds, strict=True)):
            results[k] = Stored(hold, results[k], store_sems.at[n])
        kernel(*operands, *results, *refs[2:])
        for k in far:
            operands[k].wait()
        for k in away:
            if not results[k].waited:
                results[k].wait()

    return pl.pallas_call(
        body,
        out_shape=[jax.ShapeDtypeStruct(s, t) for s, t in outs],
        in_specs=specs,
        out_specs=[plain.get(k, HBM) for k in range(len(outs))],
        scratch_shapes=held + [dma((max(sum(counts), 1),)), dma((len(away),))] + list(scratch),
        compiler_params=pltpu.CompilerParams(vmem_limit_bytes=room),
        cost_estimate=pl.CostEstimate(flops=flops, bytes_accessed=moved, transcendentals=0),
        name=name,
    )(*ins)


def exchange(x):
    return lax.all_to_all(x, AXES, split_axis=0, concat_axis=0, tiled=True)


def local(features, cotangent, w_self, w_neigh, bias, src_slot, dst_slot, edge_live, mirror_list):
    line = mirror_list.reshape(1, MIRRORS)
    lists = mirror_list[0].T
    square = ((1024, 1024), BF16)
    payload = ((PEERS, 16, F), BF16)

    edges = (EDGES // LANES, LANES)
    src, dst = src_slot.reshape(edges), dst_slot.reshape(edges)
    rows_f32, rows_bf16 = ((1024, F), F32), ((1024, F), BF16)
    out1, code = call(
        pull_kernel,
        (edge_live, lists, src, dst, features),
        [payload, (edges, jnp.int32)],
        "pull",
        scalars=(0,),
        scratch=[pltpu.VMEM((32, EDGES), BF16), pltpu.VMEM((32, EDGES), BF16)],
    )
    got1 = exchange(out1)
    quarters = [pltpu.VMEM(*square), pltpu.VMEM(*square)]
    words, gm, gg, sums, flag, mm, mg = call(
        build_kernel,
        (edge_live, code, features),
        [
            ((2 * MASTERS, LANES), jnp.int32),
            square,
            square,
            rows_f32,
            ((1,), jnp.int32),
            square,
            square,
        ],
        "build",
        scalars=(0,),
        bare=(1,),
        plain={4: SMEM, 5: HBM, 6: HBM},
        scratch=[pltpu.SMEM(edges, jnp.int32), pltpu.SemaphoreType.DMA]
        + quarters
        + [pltpu.VMEM((WORDS, 1, LANES), jnp.int32) for _ in range(COPIES)],
        flops=20_000_000_000,
        moved=20_000_000,
    )
    (out2,) = call(
        push_kernel,
        (got1, sums, gg),
        [((PEERS, 8, F), BF16)],
        "push",
        near=(0,),
        room=55_400_000,
        parts={2: PARTS},
    )
    got2 = exchange(out2)
    turned, told, sums_m, tally = call(
        local_kernel,
        (flag, got1, features, words, mm, mg),
        [((F, MASTERS), BF16), rows_bf16, rows_f32, rows_bf16],
        "local",
        scalars=(0,),
        bare=(4, 5),
        scratch=quarters + [pltpu.SemaphoreType.DMA],
        flops=2_000_000_000,
        moved=6_000_000,
    )
    act, own, msg, out3, total = call(
        dense_kernel,
        (
            got2, line, told, tally, sums_m, features, w_self, w_neigh, bias.reshape(1, H),
            cotangent, turned,
        ),
        [((MASTERS, H), BF16), rows_f32, rows_f32, payload, ((8, F), F32)],
        "dense",
        near=(0,),
        room=55_800_000,
    )
    got3 = exchange(out3)
    turned_gg, mirror, base = call(
        back_local_kernel,
        (flag, gg, msg, words, own, mm, mg),
        [square, rows_f32, rows_f32],
        "back_local",
        scalars=(0,),
        bare=(5, 6),
        scratch=quarters + [pltpu.SemaphoreType.DMA],
        flops=2_000_000_000,
        moved=6_000_000,
    )
    (out4,) = call(
        back_push_kernel,
        (got3, mirror, total, turned_gg),
        [payload],
        "back_push",
        near=(0,),
        room=55_200_000,
        parts={3: PARTS},
    )
    got4 = exchange(out4)
    (base2,) = call(
        back_mirror_kernel,
        (got3, gm, base),
        [rows_f32],
        "back_mirror",
        flops=2_000_000_000,
        moved=6_000_000,
    )
    grad_features, grad_self, grad_neigh, bias_out = call(
        last_kernel,
        (line, got4, base2),
        [rows_bf16, ((F, H), F32), ((F, H), F32), ((2, F), F32)],
        "last",
        near=(1,),
        room=55_700_000,
    )
    return act, grad_features, grad_self, grad_neigh, bias_out.reshape(H)


def solution(mesh):
    placed = (
        P(AXES, None),
        P(AXES, None),
        P(),
        P(),
        P(),
        P(AXES),
        P(AXES),
        P(AXES),
        P(AXES, None, None),
    )
    return jax.shard_map(
        local,
        mesh=mesh,
        in_specs=placed,
        out_specs=(P(AXES, None), P(AXES, None), P(), P(), P()),
        check_vma=False,
    )
```

```python
import jax
import jax.numpy as jnp
from jax import lax
from jax.experimental import pallas as pl
from jax.experimental.pallas import tpu as pltpu
from jax.sharding import PartitionSpec as P

F32 = jnp.float32
BF16 = jnp.bfloat16
AXES = ("row", "col")

MASTERS = 1024
MIRRORS = 1024
SLOTS = MASTERS + MIRRORS
EDGES = 8192
PEERS = 128
F = 128
H = 256
LANES = 128
COPIES = 6
TURN = 256
PARTS = 4
WORDS = SLOTS * (SLOTS // 1024)


def part_of(size, k, parts=PARTS):
    return pl.ds(k * (size // parts), size // parts)


def dot(a, b):
    return jnp.dot(a, b, preferred_element_type=F32)


def dot_nt(a, b):
    return lax.dot_general(a, b, (((1,), (1,)), ((), ())), preferred_element_type=F32)


def gather_matrix(column):
    places = lax.broadcasted_iota(jnp.int32, (MIRRORS, MASTERS), 1)
    return jnp.where(places == column, 1.0, 0.0).astype(BF16)


def scatter_part(line, c, parts=PARTS):
    size = MASTERS // parts
    places = lax.broadcasted_iota(jnp.int32, (size, MIRRORS), 0) + c * size
    return jnp.where(places == line, 1.0, 0.0).astype(BF16)


def pick(slots, first):
    shape = (PEERS, 8, slots.shape[1])
    spread = jnp.broadcast_to(slots[:, None, :], shape)
    wanted = first + lax.broadcasted_iota(jnp.int32, shape, 1)
    here = lax.broadcasted_iota(jnp.int32, shape, 2) == wanted
    return jnp.sum(jnp.where(here, spread, 0.0), axis=2, keepdims=True)


def as_column(lists):
    return pick(jnp.transpose(lists.astype(F32)), 0).reshape(MIRRORS, 1).astype(jnp.int32)


def numbers():
    shape = (EDGES // LANES, LANES)
    row = lax.broadcasted_iota(jnp.int32, shape, 0) * LANES
    return row + lax.broadcasted_iota(jnp.int32, shape, 1)


def pull_kernel(
    live_ref, lists_ref, src_ref, dst_ref, rows_ref, out_ref, code_ref, high_ref, low_ref
):
    gather = gather_matrix(as_column(lists_ref[...]))
    src, dst = src_ref[...], dst_ref[...]
    live = numbers() < live_ref[0]
    place = ((src >> 7) & 1) * SLOTS + dst
    code = place | ((src & 127) << 12) | ((src >> 8) << 22)
    code_ref[...] = jnp.where(live, code, 128 << 12)
    code_ref.send()
    slot = jnp.where(live, dst - MASTERS, -1)
    high, low = slot >> 5, slot & 31
    places = lax.broadcasted_iota(jnp.int32, (32, LANES), 0)
    for k in range(EDGES // LANES):
        at = pl.ds(k * LANES, LANES)
        high_ref[:, at] = jnp.where(places == high[k : k + 1], 1.0, 0.0).astype(BF16)
        low_ref[:, at] = jnp.where(places == low[k : k + 1], 1.0, 0.0).astype(BF16)
    counts = dot_nt(high_ref[...], low_ref[...])
    peer = lax.broadcasted_iota(jnp.int32, (PEERS, 32), 0)
    of_peer = jnp.where(peer >> 2 == lax.broadcasted_iota(jnp.int32, (PEERS, 32), 1), 1.0, 0.0)
    counts = sum(dot(of_peer.astype(BF16), part.astype(BF16)) for part in split(counts))
    peer = lax.broadcasted_iota(jnp.int32, (PEERS, 8, 32), 0)
    tally = jnp.broadcast_to(pick(counts, (peer & 3) << 3), (PEERS, 8, LANES))
    high, rest = split(tally)
    left = lax.broadcasted_iota(jnp.int32, tally.shape, 2) < LANES // 2
    tally = jnp.where(left, high, rest)
    rows = rows_ref[...]
    for c in range(2):
        picked = dot(gather[c * 512 : (c + 1) * 512], rows).reshape(PEERS // 2, 8, F)
        half = pl.ds(c * (PEERS // 2), PEERS // 2)
        both = [picked, tally[c * (PEERS // 2) : (c + 1) * (PEERS // 2)]]
        out_ref[half] = jnp.concatenate(both, axis=1).astype(BF16)
        out_ref.send(half)


def fours(x):
    yield x & 15
    for q in range(1, 7):
        yield lax.shift_right_logical(x, 4 * q) & 15
    yield lax.shift_right_logical(x, 28)


def put(near_ref, far_ref, row, j, counts):
    for q, count in enumerate(counts):
        half = near_ref if q < 4 else far_ref
        left = (q % 4) * 256 + j * LANES
        half[pl.ds(row, 128), pl.ds(left, LANES)] = count.astype(F32).astype(BF16)


def load_masters(flag_ref, words_ref, mm_hbm, mg_hbm, mm, mg, sem):
    words_ref.wait()

    @pl.when(flag_ref[0] == 0)
    def _():
        def block(i, carry):
            d = pl.multiple_of(i * 128, 128)
            for j in range(2):
                at = pl.ds(pl.multiple_of(j * MASTERS + d, 128), 128)
                put(mm, mg, d, j, fours(words_ref[at, :]))
            return carry

        lax.fori_loop(0, MASTERS // 128, block, 0)

    @pl.when(flag_ref[0] != 0)
    def _():
        for source, target in ((mm_hbm, mm), (mg_hbm, mg)):
            copy = pltpu.make_async_copy(source, target, sem)
            copy.start()
            copy.wait()


def build_kernel(
    live_ref, code_ref, rows_ref, words_ref, gm_ref, gg_ref, sums_ref, flag_ref, mm_hbm, mg_hbm,
    codes, sem, mm, mg, *tables3
):
    load = pltpu.make_async_copy(code_ref, codes, sem)
    load.start()
    tables = [t.reshape(WORDS, LANES) for t in tables3]
    n = live_ref[0]

    def clear(i, carry):
        for t in tables:
            t[pl.ds(pl.multiple_of(i * 256, 256), 256), :] = jnp.zeros((256, LANES), jnp.int32)
        return carry

    lax.fori_loop(0, WORDS // 256, clear, 0)
    load.wait()

    lanes = lax.broadcasted_iota(jnp.int32, (1, LANES), 1) << 12
    one = jnp.ones((1, LANES), jnp.int32)

    def code_at(k, i):
        row, lane = divmod(k, LANES)
        part = codes.at[pl.ds(row, EDGES // LANES - TURN // LANES + 1), pl.ds(lane, 1)]
        return part[i * (TURN // LANES), 0]

    def turn(i, carry):
        for start in range(0, TURN, COPIES):
            count = min(COPIES, TURN - start)
            words = [code_at(start + k, i) for k in range(count)]
            where = [w & (WORDS - 1) for w in words]
            adds = []
            for w in words:
                w = jnp.full((1, LANES), w, jnp.int32)
                bit = lax.shift_left(one, lax.shift_right_logical(w, 20))
                adds.append(jnp.where(lanes == (w & (255 << 12)), bit, 0))
            olds = [tables3[k][where[k]] for k in range(count)]
            for k in range(count):
                tables3[k][where[k]] = olds[k] + adds[k]
        return carry

    turns = (n + TURN - 1) // TURN
    lax.fori_loop(0, turns, turn, 0)

    rows = rows_ref[...]
    none = jnp.zeros((8, LANES), jnp.int32)

    def add_up(x):
        return jnp.sum(x.reshape(16, 8, LANES), axis=0)

    def table_sum(j, row):
        at = pl.ds(pl.multiple_of(j * SLOTS + row, 128), 128)
        x = tables[0][at, :]
        for t in tables[1:]:
            x = x + t[at, :]
        return x

    def mirrors(i, seen):
        e = pl.multiple_of(i * 256, 256)
        for h in range(2):
            d = pl.multiple_of(i * 256 + h * 128, 128)
            for j in range(2):
                counts = list(fours(table_sum(j, MASTERS + d)))
                put(gm_ref, gg_ref, d, j, counts)
                for count in counts:
                    seen = seen + add_up(count)
        gg_ref.send(pl.ds(e, 256))
        gm_ref.send(pl.ds(e, 256))
        return seen

    def masters(i, seen):
        e = pl.multiple_of(i * 256, 256)
        sums_ref[pl.ds(e, 256), :] = dot(gm_ref[pl.ds(e, 256), :], rows)
        for j in range(2):
            for h in range(2):
                x = table_sum(j, pl.multiple_of(i * 256 + h * 128, 128))
                words_ref[pl.ds(pl.multiple_of(j * MASTERS + e + h * 128, 128), 128), :] = x
                pairs = (x & 0x0F0F0F0F) + (lax.shift_right_logical(x, 4) & 0x0F0F0F0F)
                fourth = (pairs & 0x00FF00FF) + (lax.shift_right_logical(pairs, 8) & 0x00FF00FF)
                seen = seen + add_up(fourth)
            words_ref.send(pl.ds(pl.multiple_of(j * MASTERS + e, 256), 256))
        return seen

    def finish():
        sums_ref.send()
        for ref in (words_ref, gm_ref, gg_ref, sums_ref):
            ref.wait()

    seen = lax.fori_loop(0, MIRRORS // 256, mirrors, none)
    halves = lax.fori_loop(0, MASTERS // 256, masters, none)
    seen = seen + (halves & 0xFFFF) + lax.shift_right_logical(halves, 16)
    found = jnp.sum(seen.astype(F32))
    finish()
    flag_ref[0] = jnp.where(found != n.astype(F32), 1, 0)

    @pl.when(found != n.astype(F32))
    def _():
        lax.fori_loop(0, WORDS // 256, clear, 0)

        def edge(e, carry):
            word = codes[e // LANES, e % LANES]
            at = word & (WORDS - 1)
            q = word >> 22
            one = jnp.where(lanes == (word & (127 << 12)), jnp.where(q >= 4, 65536, 1), 0)
            for k in range(4):
                tables3[k][at] = tables3[k][at] + jnp.where(q % 4 == k, one, 0)
            return carry

        lax.fori_loop(0, n, edge, 0)

        def wide(j, row):
            at = pl.ds(pl.multiple_of(j * SLOTS + row, 128), 128)
            found = [t[at, :] for t in tables[:4]]
            return [x & 65535 for x in found] + [lax.shift_right_logical(x, 16) for x in found]

        def block(i, carry):
            d = pl.multiple_of(i * 128, 128)
            for j in range(2):
                put(gm_ref, gg_ref, d, j, wide(j, MASTERS + d))
                put(mm, mg, d, j, wide(j, d))
            sums_ref[pl.ds(d, 128), :] = dot(gm_ref[pl.ds(d, 128), :], rows)
            return carry

        lax.fori_loop(0, MASTERS // 128, block, 0)
        words_ref.send()
        gm_ref.send()
        gg_ref.send()
        finish()
        for source, target in ((mm, mm_hbm), (mg, mg_hbm)):
            copy = pltpu.make_async_copy(source, target, sem)
            copy.start()
            copy.wait()


def split(x):
    high = x.astype(BF16).astype(F32)
    return high, (x - high).astype(BF16).astype(F32)


def parts_of(got):
    got = got.astype(F32)
    return got[:, :8].reshape(MIRRORS, F).astype(BF16), got[:, 8:]


def two_parts(x):
    high, low = split(x)
    left = lax.broadcasted_iota(jnp.int32, x.shape, 1) < LANES // 2
    return jnp.where(left, high, low).astype(BF16)


def push_kernel(got_ref, sums_ref, gg_ref, out_ref):
    got, _ = parts_of(got_ref[...])
    for c in range(PARTS):
        rows, peers = part_of(MIRRORS, c), part_of(PEERS, c)
        sums = dot(gg_ref.part(c), got) + sums_ref[rows]
        out_ref[peers] = sums.reshape(PEERS // PARTS, 8, F).astype(BF16)
        out_ref.send(peers)


def local_kernel(
    flag_ref, got_ref, rows_ref, words_ref, mm_hbm, mg_hbm,
    turned_ref, told_ref, sums_ref, tally_ref, mm, mg, sem,
):
    rows = rows_ref[...]
    turned_ref[...] = rows.astype(F32).T.astype(BF16)
    turned_ref.send()
    both = got_ref[...].astype(F32)
    both = [both[:, :8].reshape(MIRRORS, F), both[:, 8:].reshape(MIRRORS, LANES)]
    both = jnp.concatenate(both, axis=1).astype(BF16)
    told_ref[...] = both[:, F:]
    told_ref.send()
    ones = jnp.ones((MASTERS, LANES), BF16)
    near = jnp.concatenate([rows, ones], axis=1)
    far = jnp.concatenate([both[:, :F], ones], axis=1)
    load_masters(flag_ref, words_ref, mm_hbm, mg_hbm, mm, mg, sem)
    both = dot(mg[...], far) + dot(mm[...], near)
    sums_ref[...] = both[:, :F]
    sums_ref.send()
    tally_ref[...] = two_parts(both[:, F:])
    tally_ref.send()


def dense_kernel(
    got_ref, line_ref, told_ref, tally_ref, sums_ref, rows_ref, self_ref, neigh_ref, bias_ref,
    cot_ref, turned_ref,
    act_ref, own_ref, msg_ref, out_ref, total_ref,
):
    line = line_ref[...]
    wide = jnp.concatenate([got_ref[...].reshape(MIRRORS, F), told_ref[...]], axis=1)
    w = jnp.concatenate([self_ref[...], neigh_ref[...]], axis=0)
    bias = bias_ref[...]
    size = MASTERS // 2
    scatters = [scatter_part(line, c, 2) for c in range(2)]
    folds = [dot(scatter, wide) for scatter in scatters]
    terms, total, picked = 0.0, 0.0, 0.0
    for c in range(2):
        rows, scatter, folded = part_of(MASTERS, c, 2), scatters[c], folds[c]
        degree = folded[:, F:] + tally_ref[rows].astype(F32)
        degree = degree + pltpu.roll(degree, LANES // 2, 1)
        inverse = 1.0 / jnp.maximum(degree, 1.0)
        mean = (sums_ref[rows] + folded[:, :F]) * inverse
        pre = dot(jnp.concatenate([rows_ref[rows], mean.astype(BF16)], axis=1), w) + bias
        sig = jax.nn.sigmoid(pre)
        act_ref[rows] = (pre * sig).astype(BF16)
        grad = (cot_ref[rows].astype(F32) * sig * (1.0 + pre * (1.0 - sig))).astype(BF16)
        back = dot_nt(grad, w)
        own_ref[rows] = back[:, :F]
        msg = back[:, F:] * inverse
        msg_ref[rows] = msg
        for ref in (act_ref, own_ref, msg_ref):
            ref.send(rows)
        picked = picked + dot(msg.T.astype(BF16), scatter)
        turned = [turned_ref[:, c * size : (c + 1) * size], mean.T.astype(BF16)]
        terms = terms + dot(jnp.concatenate(turned, axis=0), grad)
        total = total + dot(jnp.ones((8, size), BF16), grad)
    flat = jnp.concatenate([terms[:, :F], terms[:, F:]], axis=0).reshape(PEERS // 2, 8, F)
    high, low = split(flat)
    first = lax.broadcasted_iota(jnp.int32, (PEERS // 2, 8, F), 1) < 4
    even = jnp.where(first, high, pltpu.roll(low, 4, 1))
    odd = jnp.where(first, pltpu.roll(high, 4, 1), low)
    mixed = jnp.stack([even, odd], axis=1).reshape(PEERS, 8, F)
    for c in range(2):
        peers, count = part_of(PEERS, c, 2), PEERS // 2
        rows = picked[:, c * 8 * count : (c + 1) * 8 * count].T.reshape(count, 8, F)
        both = [rows, mixed[c * count : (c + 1) * count]]
        out_ref[peers] = jnp.concatenate(both, axis=1).astype(BF16)
        out_ref.send(peers)
    high, low = split(total)
    sub = lax.broadcasted_iota(jnp.int32, (8, F), 0)
    tile = jnp.where(sub == 4, high[:, :F], 0.0)
    tile = jnp.where(sub == 5, high[:, F:], tile)
    tile = jnp.where(sub == 6, low[:, :F], tile)
    total_ref[...] = jnp.where(sub == 7, low[:, F:], tile)
    total_ref.send()


def back_local_kernel(
    flag_ref, gg_ref, msg_ref, words_ref, own_ref, mm_hbm, mg_hbm,
    turned_ref, mirror_ref, base_ref, mm, mg, sem,
):
    turned_ref[...] = gg_ref[...].T
    turned_ref.send()
    msg = msg_ref[...].T.astype(BF16)
    load_masters(flag_ref, words_ref, mm_hbm, mg_hbm, mm, mg, sem)
    mirror_ref[...] = dot(msg, mg[...]).T
    mirror_ref.send()
    base_ref[...] = dot(msg, mm[...]).T + own_ref[...]
    base_ref.send()


def back_push_kernel(got_ref, mirror_ref, total_ref, turned_ref, out_ref):
    rows, terms = parts_of(got_ref[...])
    total = jnp.sum(terms, axis=0)
    total = total + pltpu.roll(total, 4, 0)
    sub = lax.broadcasted_iota(jnp.int32, (8, F), 0)
    tile = jnp.where(sub < 4, total, total_ref[...])
    shape = (PEERS // PARTS, 8, F)
    tiles = jnp.broadcast_to(tile[None], shape)
    for c in range(PARTS):
        peers = part_of(PEERS, c)
        spread = dot(turned_ref.part(c), rows) + mirror_ref[part_of(MIRRORS, c)]
        out_ref[peers] = jnp.concatenate([spread.reshape(shape), tiles], axis=1).astype(BF16)
        out_ref.send(peers)


def back_mirror_kernel(got_ref, gm_ref, base_ref, out_ref):
    turned = got_ref[...].astype(F32)[:, :8].reshape(MIRRORS, F).T.astype(BF16)
    out_ref[...] = dot(turned, gm_ref[...]).T + base_ref[...]
    out_ref.send()


def last_kernel(line_ref, got_ref, base_ref, grad_ref, self_ref, neigh_ref, bias_ref):
    rows, tiles = parts_of(got_ref[...])
    line = line_ref[...]
    for c in range(PARTS):
        part = part_of(MASTERS, c)
        grad_ref[part] = (dot(scatter_part(line, c), rows) + base_ref[part]).astype(BF16)
        grad_ref.send(part)
    pairs = tiles.reshape(PEERS // 2, 2, 8, F)
    first = lax.broadcasted_iota(jnp.int32, (PEERS // 2, 8, F), 1) < 4
    flat = jnp.where(first, pairs[:, 0], pltpu.roll(pairs[:, 1], 4, 1)).reshape(2 * H, F)
    self_ref[:, :F] = flat[:F]
    self_ref[:, F:] = flat[H : H + F]
    neigh_ref[:, :F] = flat[F:H]
    neigh_ref[:, F:] = flat[H + F :]
    total = jnp.sum(tiles, axis=0)
    bias_ref[...] = total[4:6] + total[6:8]
    for ref in (self_ref, neigh_ref, bias_ref):
        ref.send()


VMEM = pl.BlockSpec(memory_space=pltpu.VMEM)
SMEM = pl.BlockSpec(memory_space=pltpu.SMEM)
HBM = pl.BlockSpec(memory_space=pltpu.HBM)
ALL = 60 * 1024 * 1024


class Loaded:
    def __init__(self, source, held, sems, first, parts):
        size = held.shape[0] // parts
        self.held, self.size = held, size
        self.copies = []
        for k in range(parts):
            rows = pl.ds(k * size, size)
            copy = pltpu.make_async_copy(source.at[rows], held.at[rows], sems.at[first + k])
            copy.start()
            self.copies.append(copy)

    def part(self, k):
        if self.copies[k] is not None:
            self.copies[k].wait()
            self.copies[k] = None
        return self.held[pl.ds(k * self.size, self.size)]

    def wait(self):
        for k, copy in enumerate(self.copies):
            if copy is not None:
                copy.wait()
                self.copies[k] = None

    def __getitem__(self, at):
        self.wait()
        return self.held[at]


class Stored:
    def __init__(self, held, target, sem):
        self.held, self.target, self.sem = held, target, sem
        self.copy = pltpu.make_async_copy(held, target, sem)
        self.waited = False

    def __setitem__(self, at, value):
        self.held[at] = value

    def __getitem__(self, at):
        return self.held[at]

    def wait(self):
        self.copy.wait()
        self.waited = True

    def send(self, rows=None):
        if rows is None:
            self.copy.start()
        else:
            pltpu.make_async_copy(self.held.at[rows], self.target.at[rows], self.sem).start()


def call(
    kernel, ins, outs, name, near=(), scalars=(), bare=(), plain=None, scratch=(), parts=None,
    room=ALL, flops=0, moved=0,
):
    parts, plain = parts or {}, plain or {}
    away = [k for k in range(len(outs)) if k not in plain]
    far = [k for k in range(len(ins)) if k not in (*near, *scalars, *bare)]
    specs = [VMEM if k in near else SMEM if k in scalars else HBM for k in range(len(ins))]
    held = [pltpu.VMEM(ins[k].shape, ins[k].dtype) for k in far]
    held += [pltpu.VMEM(*outs[k]) for k in away]
    counts = [parts.get(k, 1) for k in far]
    dma = pltpu.SemaphoreType.DMA

    def body(*refs):
        operands, refs = list(refs[: len(ins)]), refs[len(ins) :]
        results, refs = list(refs[: len(outs)]), refs[len(outs) :]
        copies, refs = refs[: len(far)], refs[len(far) :]
        holds, refs = refs[: len(away)], refs[len(away) :]
        load_sems, store_sems = refs[0], refs[1]
        first = 0
        for k, copy, count in zip(far, copies, counts, strict=True):
            operands[k] = Loaded(operands[k], copy, load_sems, first, count)
            first += count
        for n, (k, hold) in enumerate(zip(away, holds, strict=True)):
            results[k] = Stored(hold, results[k], store_sems.at[n])
        kernel(*operands, *results, *refs[2:])
        for k in far:
            operands[k].wait()
        for k in away:
            if not results[k].waited:
                results[k].wait()

    return pl.pallas_call(
        body,
        out_shape=[jax.ShapeDtypeStruct(s, t) for s, t in outs],
        in_specs=specs,
        out_specs=[plain.get(k, HBM) for k in range(len(outs))],
        scratch_shapes=held + [dma((max(sum(counts), 1),)), dma((len(away),))] + list(scratch),
        compiler_params=pltpu.CompilerParams(vmem_limit_bytes=room),
        cost_estimate=pl.CostEstimate(flops=flops, bytes_accessed=moved, transcendentals=0),
        name=name,
    )(*ins)


def exchange(x):
    return lax.all_to_all(x, AXES, split_axis=0, concat_axis=0, tiled=True)


def local(features, cotangent, w_self, w_neigh, bias, src_slot, dst_slot, edge_live, mirror_list):
    line = mirror_list.reshape(1, MIRRORS)
    lists = mirror_list[0].T
    square = ((1024, 1024), BF16)
    payload = ((PEERS, 16, F), BF16)

    edges = (EDGES // LANES, LANES)
    src, dst = src_slot.reshape(edges), dst_slot.reshape(edges)
    rows_f32, rows_bf16 = ((1024, F), F32), ((1024, F), BF16)
    out1, code = call(
        pull_kernel,
        (edge_live, lists, src, dst, features),
        [payload, (edges, jnp.int32)],
        "pull",
        scalars=(0,),
        scratch=[pltpu.VMEM((32, EDGES), BF16), pltpu.VMEM((32, EDGES), BF16)],
    )
    got1 = exchange(out1)
    quarters = [pltpu.VMEM(*square), pltpu.VMEM(*square)]
    words, gm, gg, sums, flag, mm, mg = call(
        build_kernel,
        (edge_live, code, features),
        [
            ((2 * MASTERS, LANES), jnp.int32),
            square,
            square,
            rows_f32,
            ((1,), jnp.int32),
            square,
            square,
        ],
        "build",
        scalars=(0,),
        bare=(1,),
        plain={4: SMEM, 5: HBM, 6: HBM},
        scratch=[pltpu.SMEM(edges, jnp.int32), pltpu.SemaphoreType.DMA]
        + quarters
        + [pltpu.VMEM((WORDS, 1, LANES), jnp.int32) for _ in range(COPIES)],
        flops=20_000_000_000,
        moved=20_000_000,
    )
    (out2,) = call(
        push_kernel,
        (got1, sums, gg),
        [((PEERS, 8, F), BF16)],
        "push",
        near=(0,),
        room=55_400_000,
        parts={2: PARTS},
    )
    got2 = exchange(out2)
    turned, told, sums_m, tally = call(
        local_kernel,
        (flag, got1, features, words, mm, mg),
        [((F, MASTERS), BF16), rows_bf16, rows_f32, rows_bf16],
        "local",
        room=55_000_000,
        scalars=(0,),
        bare=(4, 5),
        scratch=quarters + [pltpu.SemaphoreType.DMA],
        flops=2_000_000_000,
        moved=6_000_000,
    )
    act, own, msg, out3, total = call(
        dense_kernel,
        (
            got2, line, told, tally, sums_m, features, w_self, w_neigh, bias.reshape(1, H),
            cotangent, turned,
        ),
        [((MASTERS, H), BF16), rows_f32, rows_f32, payload, ((8, F), F32)],
        "dense",
        near=(0,),
        room=55_000_000,
    )
    got3 = exchange(out3)
    turned_gg, mirror, base = call(
        back_local_kernel,
        (flag, gg, msg, words, own, mm, mg),
        [square, rows_f32, rows_f32],
        "back_local",
        scalars=(0,),
        bare=(5, 6),
        scratch=quarters + [pltpu.SemaphoreType.DMA],
        flops=2_000_000_000,
        moved=6_000_000,
    )
    (out4,) = call(
        back_push_kernel,
        (got3, mirror, total, turned_gg),
        [payload],
        "back_push",
        near=(0,),
        room=55_200_000,
        parts={3: PARTS},
    )
    got4 = exchange(out4)
    (base2,) = call(
        back_mirror_kernel,
        (got3, gm, base),
        [rows_f32],
        "back_mirror",
        flops=2_000_000_000,
        moved=6_000_000,
    )
    grad_features, grad_self, grad_neigh, bias_out = call(
        last_kernel,
        (line, got4, base2),
        [rows_bf16, ((F, H), F32), ((F, H), F32), ((2, F), F32)],
        "last",
        near=(1,),
        room=55_700_000,
    )
    return act, grad_features, grad_self, grad_neigh, bias_out.reshape(H)


def solution(mesh):
    placed = (
        P(AXES, None),
        P(AXES, None),
        P(),
        P(),
        P(),
        P(AXES),
        P(AXES),
        P(AXES),
        P(AXES, None, None),
    )
    return jax.shard_map(
        local,
        mesh=mesh,
        in_specs=placed,
        out_specs=(P(AXES, None), P(AXES, None), P(), P(), P()),
        check_vma=False,
    )
```

```python
import jax
import jax.numpy as jnp
from jax import lax
from jax.experimental import pallas as pl
from jax.experimental.pallas import tpu as pltpu
from jax.sharding import PartitionSpec as P

F32 = jnp.float32
BF16 = jnp.bfloat16
AXES = ("row", "col")

MASTERS = 1024
MIRRORS = 1024
SLOTS = MASTERS + MIRRORS
EDGES = 8192
PEERS = 128
F = 128
H = 256
LANES = 128
COPIES = 6
TURN = 256
PARTS = 4
WORDS = SLOTS * (SLOTS // 1024)


def part_of(size, k, parts=PARTS):
    return pl.ds(k * (size // parts), size // parts)


def dot(a, b):
    return jnp.dot(a, b, preferred_element_type=F32)


def dot_nt(a, b):
    return lax.dot_general(a, b, (((1,), (1,)), ((), ())), preferred_element_type=F32)


def gather_matrix(column):
    places = lax.broadcasted_iota(jnp.int32, (MIRRORS, MASTERS), 1)
    return jnp.where(places == column, 1.0, 0.0).astype(BF16)


def scatter_part(line, c, parts=PARTS):
    size = MASTERS // parts
    places = lax.broadcasted_iota(jnp.int32, (size, MIRRORS), 0) + c * size
    return jnp.where(places == line, 1.0, 0.0).astype(BF16)


def pick(slots, first):
    shape = (PEERS, 8, slots.shape[1])
    spread = jnp.broadcast_to(slots[:, None, :], shape)
    wanted = first + lax.broadcasted_iota(jnp.int32, shape, 1)
    here = lax.broadcasted_iota(jnp.int32, shape, 2) == wanted
    return jnp.sum(jnp.where(here, spread, 0.0), axis=2, keepdims=True)


def as_column(lists):
    return pick(jnp.transpose(lists.astype(F32)), 0).reshape(MIRRORS, 1).astype(jnp.int32)


def numbers():
    shape = (EDGES // LANES, LANES)
    row = lax.broadcasted_iota(jnp.int32, shape, 0) * LANES
    return row + lax.broadcasted_iota(jnp.int32, shape, 1)


def pull_kernel(
    live_ref, lists_ref, src_ref, dst_ref, rows_ref, out_ref, code_ref, high_ref, low_ref
):
    gather = gather_matrix(as_column(lists_ref[...]))
    src, dst = src_ref[...], dst_ref[...]
    live = numbers() < live_ref[0]
    place = ((src >> 7) & 1) * SLOTS + dst
    code = place | ((src & 127) << 12) | ((src >> 8) << 22)
    code_ref[...] = jnp.where(live, code, 128 << 12)
    code_ref.send()
    slot = jnp.where(live, dst - MASTERS, -1)
    high, low = slot >> 5, slot & 31
    places = lax.broadcasted_iota(jnp.int32, (32, LANES), 0)
    for k in range(EDGES // LANES):
        at = pl.ds(k * LANES, LANES)
        high_ref[:, at] = jnp.where(places == high[k : k + 1], 1.0, 0.0).astype(BF16)
        low_ref[:, at] = jnp.where(places == low[k : k + 1], 1.0, 0.0).astype(BF16)
    counts = dot_nt(high_ref[...], low_ref[...])
    peer = lax.broadcasted_iota(jnp.int32, (PEERS, 32), 0)
    of_peer = jnp.where(peer >> 2 == lax.broadcasted_iota(jnp.int32, (PEERS, 32), 1), 1.0, 0.0)
    counts = sum(dot(of_peer.astype(BF16), part.astype(BF16)) for part in split(counts))
    peer = lax.broadcasted_iota(jnp.int32, (PEERS, 8, 32), 0)
    tally = jnp.broadcast_to(pick(counts, (peer & 3) << 3), (PEERS, 8, LANES))
    high, rest = split(tally)
    left = lax.broadcasted_iota(jnp.int32, tally.shape, 2) < LANES // 2
    tally = jnp.where(left, high, rest)
    rows = rows_ref[...]
    for c in range(2):
        picked = dot(gather[c * 512 : (c + 1) * 512], rows).reshape(PEERS // 2, 8, F)
        half = pl.ds(c * (PEERS // 2), PEERS // 2)
        both = [picked, tally[c * (PEERS // 2) : (c + 1) * (PEERS // 2)]]
        out_ref[half] = jnp.concatenate(both, axis=1).astype(BF16)
        out_ref.send(half)


def fours(x):
    yield x & 15
    for q in range(1, 7):
        yield lax.shift_right_logical(x, 4 * q) & 15
    yield lax.shift_right_logical(x, 28)


def put(near_ref, far_ref, row, j, counts):
    for q, count in enumerate(counts):
        half = near_ref if q < 4 else far_ref
        left = (q % 4) * 256 + j * LANES
        half[pl.ds(row, 128), pl.ds(left, LANES)] = count.astype(F32).astype(BF16)


def load_masters(flag_ref, words_ref, mm_hbm, mg_hbm, mm, mg, sem):
    words_ref.wait()

    @pl.when(flag_ref[0] == 0)
    def _():
        def block(i, carry):
            d = pl.multiple_of(i * 128, 128)
            for j in range(2):
                at = pl.ds(pl.multiple_of(j * MASTERS + d, 128), 128)
                put(mm, mg, d, j, fours(words_ref[at, :]))
            return carry

        lax.fori_loop(0, MASTERS // 128, block, 0)

    @pl.when(flag_ref[0] != 0)
    def _():
        for source, target in ((mm_hbm, mm), (mg_hbm, mg)):
            copy = pltpu.make_async_copy(source, target, sem)
            copy.start()
            copy.wait()


def build_kernel(
    live_ref, code_ref, rows_ref, words_ref, gm_ref, gg_ref, sums_ref, flag_ref, mm_hbm, mg_hbm,
    codes, sem, mm, mg, *tables3
):
    load = pltpu.make_async_copy(code_ref, codes, sem)
    load.start()
    tables = [t.reshape(WORDS, LANES) for t in tables3]
    n = live_ref[0]

    def clear(i, carry):
        for t in tables:
            t[pl.ds(pl.multiple_of(i * 256, 256), 256), :] = jnp.zeros((256, LANES), jnp.int32)
        return carry

    lax.fori_loop(0, WORDS // 256, clear, 0)
    load.wait()

    lanes = lax.broadcasted_iota(jnp.int32, (1, LANES), 1) << 12
    one = jnp.ones((1, LANES), jnp.int32)

    def code_at(k, i):
        row, lane = divmod(k, LANES)
        part = codes.at[pl.ds(row, EDGES // LANES - TURN // LANES + 1), pl.ds(lane, 1)]
        return part[i * (TURN // LANES), 0]

    def turn(i, carry):
        for start in range(0, TURN, COPIES):
            count = min(COPIES, TURN - start)
            words = [code_at(start + k, i) for k in range(count)]
            where = [w & (WORDS - 1) for w in words]
            adds = []
            for w in words:
                w = jnp.full((1, LANES), w, jnp.int32)
                bit = lax.shift_left(one, lax.shift_right_logical(w, 20))
                adds.append(jnp.where(lanes == (w & (255 << 12)), bit, 0))
            olds = [tables3[k][where[k]] for k in range(count)]
            for k in range(count):
                tables3[k][where[k]] = olds[k] + adds[k]
        return carry

    turns = (n + TURN - 1) // TURN
    lax.fori_loop(0, turns, turn, 0)

    rows = rows_ref[...]
    none = jnp.zeros((8, LANES), jnp.int32)

    def add_up(x):
        return jnp.sum(x.reshape(16, 8, LANES), axis=0)

    def table_sum(j, row):
        at = pl.ds(pl.multiple_of(j * SLOTS + row, 128), 128)
        x = tables[0][at, :]
        for t in tables[1:]:
            x = x + t[at, :]
        return x

    def mirrors(i, seen):
        e = pl.multiple_of(i * 256, 256)
        for h in range(2):
            d = pl.multiple_of(i * 256 + h * 128, 128)
            for j in range(2):
                counts = list(fours(table_sum(j, MASTERS + d)))
                put(gm_ref, gg_ref, d, j, counts)
                for count in counts:
                    seen = seen + add_up(count)
        gg_ref.send(pl.ds(e, 256))
        gm_ref.send(pl.ds(e, 256))
        return seen

    def masters(i, seen):
        e = pl.multiple_of(i * 256, 256)
        sums_ref[pl.ds(e, 256), :] = dot(gm_ref[pl.ds(e, 256), :], rows)
        for j in range(2):
            for h in range(2):
                x = table_sum(j, pl.multiple_of(i * 256 + h * 128, 128))
                words_ref[pl.ds(pl.multiple_of(j * MASTERS + e + h * 128, 128), 128), :] = x
                pairs = (x & 0x0F0F0F0F) + (lax.shift_right_logical(x, 4) & 0x0F0F0F0F)
                fourth = (pairs & 0x00FF00FF) + (lax.shift_right_logical(pairs, 8) & 0x00FF00FF)
                seen = seen + add_up(fourth)
            words_ref.send(pl.ds(pl.multiple_of(j * MASTERS + e, 256), 256))
        return seen

    def finish():
        sums_ref.send()
        for ref in (words_ref, gm_ref, gg_ref, sums_ref):
            ref.wait()

    seen = lax.fori_loop(0, MIRRORS // 256, mirrors, none)
    halves = lax.fori_loop(0, MASTERS // 256, masters, none)
    seen = seen + (halves & 0xFFFF) + lax.shift_right_logical(halves, 16)
    found = jnp.sum(seen.astype(F32))
    finish()
    flag_ref[0] = jnp.where(found != n.astype(F32), 1, 0)

    @pl.when(found != n.astype(F32))
    def _():
        lax.fori_loop(0, WORDS // 256, clear, 0)

        def edge(e, carry):
            word = codes[e // LANES, e % LANES]
            at = word & (WORDS - 1)
            q = word >> 22
            one = jnp.where(lanes == (word & (127 << 12)), jnp.where(q >= 4, 65536, 1), 0)
            for k in range(4):
                tables3[k][at] = tables3[k][at] + jnp.where(q % 4 == k, one, 0)
            return carry

        lax.fori_loop(0, n, edge, 0)

        def wide(j, row):
            at = pl.ds(pl.multiple_of(j * SLOTS + row, 128), 128)
            found = [t[at, :] for t in tables[:4]]
            return [x & 65535 for x in found] + [lax.shift_right_logical(x, 16) for x in found]

        def block(i, carry):
            d = pl.multiple_of(i * 128, 128)
            for j in range(2):
                put(gm_ref, gg_ref, d, j, wide(j, MASTERS + d))
                put(mm, mg, d, j, wide(j, d))
            sums_ref[pl.ds(d, 128), :] = dot(gm_ref[pl.ds(d, 128), :], rows)
            return carry

        lax.fori_loop(0, MASTERS // 128, block, 0)
        words_ref.send()
        gm_ref.send()
        gg_ref.send()
        finish()
        for source, target in ((mm, mm_hbm), (mg, mg_hbm)):
            copy = pltpu.make_async_copy(source, target, sem)
            copy.start()
            copy.wait()


def split(x):
    high = x.astype(BF16).astype(F32)
    return high, (x - high).astype(BF16).astype(F32)


def parts_of(got):
    got = got.astype(F32)
    return got[:, :8].reshape(MIRRORS, F).astype(BF16), got[:, 8:]


def two_parts(x):
    high, low = split(x)
    left = lax.broadcasted_iota(jnp.int32, x.shape, 1) < LANES // 2
    return jnp.where(left, high, low).astype(BF16)


def push_kernel(got_ref, sums_ref, gg_ref, out_ref):
    got, _ = parts_of(got_ref[...])
    for c in range(PARTS):
        rows, peers = part_of(MIRRORS, c), part_of(PEERS, c)
        sums = dot(gg_ref.part(c), got) + sums_ref[rows]
        out_ref[peers] = sums.reshape(PEERS // PARTS, 8, F).astype(BF16)
        out_ref.send(peers)


def local_kernel(
    flag_ref, got_ref, rows_ref, words_ref, mm_hbm, mg_hbm,
    turned_ref, told_ref, sums_ref, tally_ref, mm, mg, sem,
):
    rows = rows_ref[...]
    turned_ref[...] = rows.astype(F32).T.astype(BF16)
    turned_ref.send()
    both = got_ref[...].astype(F32)
    both = [both[:, :8].reshape(MIRRORS, F), both[:, 8:].reshape(MIRRORS, LANES)]
    both = jnp.concatenate(both, axis=1).astype(BF16)
    told_ref[...] = both[:, F:]
    told_ref.send()
    ones = jnp.ones((MASTERS, LANES), BF16)
    near = jnp.concatenate([rows, ones], axis=1)
    far = jnp.concatenate([both[:, :F], ones], axis=1)
    load_masters(flag_ref, words_ref, mm_hbm, mg_hbm, mm, mg, sem)
    both = dot(mg[...], far) + dot(mm[...], near)
    sums_ref[...] = both[:, :F]
    sums_ref.send()
    tally_ref[...] = two_parts(both[:, F:])
    tally_ref.send()


def dense_kernel(
    got_ref, line_ref, told_ref, tally_ref, sums_ref, rows_ref, self_ref, neigh_ref, bias_ref,
    cot_ref, turned_ref,
    act_ref, own_ref, msg_ref, out_ref, total_ref,
):
    line = line_ref[...]
    wide = jnp.concatenate([got_ref[...].reshape(MIRRORS, F), told_ref[...]], axis=1)
    w = jnp.concatenate([self_ref[...], neigh_ref[...]], axis=0)
    bias = bias_ref[...]
    size = MASTERS // 2
    scatters = [scatter_part(line, c, 2) for c in range(2)]
    folds = [dot(scatter, wide) for scatter in scatters]
    terms, total, picked = 0.0, 0.0, 0.0
    for c in range(2):
        rows, scatter, folded = part_of(MASTERS, c, 2), scatters[c], folds[c]
        degree = folded[:, F:] + tally_ref[rows].astype(F32)
        degree = degree + pltpu.roll(degree, LANES // 2, 1)
        inverse = 1.0 / jnp.maximum(degree, 1.0)
        mean = (sums_ref[rows] + folded[:, :F]) * inverse
        pre = dot(jnp.concatenate([rows_ref[rows], mean.astype(BF16)], axis=1), w) + bias
        sig = jax.nn.sigmoid(pre)
        act_ref[rows] = (pre * sig).astype(BF16)
        grad = (cot_ref[rows].astype(F32) * sig * (1.0 + pre * (1.0 - sig))).astype(BF16)
        back = dot_nt(grad, w)
        own_ref[rows] = back[:, :F]
        msg = back[:, F:] * inverse
        msg_ref[rows] = msg
        for ref in (act_ref, own_ref, msg_ref):
            ref.send(rows)
        picked = picked + dot(msg.T.astype(BF16), scatter)
        turned = [turned_ref[:, c * size : (c + 1) * size], mean.T.astype(BF16)]
        terms = terms + dot(jnp.concatenate(turned, axis=0), grad)
        total = total + dot(jnp.ones((8, size), BF16), grad)
    flat = jnp.concatenate([terms[:, :F], terms[:, F:]], axis=0).reshape(PEERS // 2, 8, F)
    high, low = split(flat)
    first = lax.broadcasted_iota(jnp.int32, (PEERS // 2, 8, F), 1) < 4
    even = jnp.where(first, high, pltpu.roll(low, 4, 1))
    odd = jnp.where(first, pltpu.roll(high, 4, 1), low)
    mixed = jnp.stack([even, odd], axis=1).reshape(PEERS, 8, F)
    for c in range(2):
        peers, count = part_of(PEERS, c, 2), PEERS // 2
        rows = picked[:, c * 8 * count : (c + 1) * 8 * count].T.reshape(count, 8, F)
        both = [rows, mixed[c * count : (c + 1) * count]]
        out_ref[peers] = jnp.concatenate(both, axis=1).astype(BF16)
        out_ref.send(peers)
    high, low = split(total)
    sub = lax.broadcasted_iota(jnp.int32, (8, F), 0)
    tile = jnp.where(sub == 4, high[:, :F], 0.0)
    tile = jnp.where(sub == 5, high[:, F:], tile)
    tile = jnp.where(sub == 6, low[:, :F], tile)
    total_ref[...] = jnp.where(sub == 7, low[:, F:], tile)
    total_ref.send()


def back_local_kernel(
    flag_ref, gg_ref, msg_ref, words_ref, own_ref, mm_hbm, mg_hbm,
    turned_ref, mirror_ref, base_ref, mm, mg, sem,
):
    turned_ref[...] = gg_ref[...].T
    turned_ref.send()
    msg = msg_ref[...].T.astype(BF16)
    load_masters(flag_ref, words_ref, mm_hbm, mg_hbm, mm, mg, sem)
    mirror_ref[...] = dot(msg, mg[...]).T
    mirror_ref.send()
    base_ref[...] = dot(msg, mm[...]).T + own_ref[...]
    base_ref.send()


def back_push_kernel(got_ref, mirror_ref, total_ref, turned_ref, out_ref):
    rows, terms = parts_of(got_ref[...])
    total = jnp.sum(terms, axis=0)
    total = total + pltpu.roll(total, 4, 0)
    sub = lax.broadcasted_iota(jnp.int32, (8, F), 0)
    tile = jnp.where(sub < 4, total, total_ref[...])
    shape = (PEERS // PARTS, 8, F)
    tiles = jnp.broadcast_to(tile[None], shape)
    for c in range(PARTS):
        peers = part_of(PEERS, c)
        spread = dot(turned_ref.part(c), rows) + mirror_ref[part_of(MIRRORS, c)]
        out_ref[peers] = jnp.concatenate([spread.reshape(shape), tiles], axis=1).astype(BF16)
        out_ref.send(peers)


def back_mirror_kernel(got_ref, gm_ref, base_ref, out_ref):
    turned = got_ref[...].astype(F32)[:, :8].reshape(MIRRORS, F).T.astype(BF16)
    out_ref[...] = dot(turned, gm_ref[...]).T + base_ref[...]
    out_ref.send()


def last_kernel(line_ref, got_ref, base_ref, grad_ref, self_ref, neigh_ref, bias_ref):
    rows, tiles = parts_of(got_ref[...])
    line = line_ref[...]
    for c in range(PARTS):
        part = part_of(MASTERS, c)
        grad_ref[part] = (dot(scatter_part(line, c), rows) + base_ref[part]).astype(BF16)
        grad_ref.send(part)
    pairs = tiles.reshape(PEERS // 2, 2, 8, F)
    first = lax.broadcasted_iota(jnp.int32, (PEERS // 2, 8, F), 1) < 4
    flat = jnp.where(first, pairs[:, 0], pltpu.roll(pairs[:, 1], 4, 1)).reshape(2 * H, F)
    self_ref[:, :F] = flat[:F]
    self_ref[:, F:] = flat[H : H + F]
    neigh_ref[:, :F] = flat[F:H]
    neigh_ref[:, F:] = flat[H + F :]
    total = jnp.sum(tiles, axis=0)
    bias_ref[...] = total[4:6] + total[6:8]
    for ref in (self_ref, neigh_ref, bias_ref):
        ref.send()


VMEM = pl.BlockSpec(memory_space=pltpu.VMEM)
SMEM = pl.BlockSpec(memory_space=pltpu.SMEM)
HBM = pl.BlockSpec(memory_space=pltpu.HBM)
ALL = 60 * 1024 * 1024


class Loaded:
    def __init__(self, source, held, sems, first, parts):
        size = held.shape[0] // parts
        self.held, self.size = held, size
        self.copies = []
        for k in range(parts):
            rows = pl.ds(k * size, size)
            copy = pltpu.make_async_copy(source.at[rows], held.at[rows], sems.at[first + k])
            copy.start()
            self.copies.append(copy)

    def part(self, k):
        if self.copies[k] is not None:
            self.copies[k].wait()
            self.copies[k] = None
        return self.held[pl.ds(k * self.size, self.size)]

    def wait(self):
        for k, copy in enumerate(self.copies):
            if copy is not None:
                copy.wait()
                self.copies[k] = None

    def __getitem__(self, at):
        self.wait()
        return self.held[at]


class Stored:
    def __init__(self, held, target, sem):
        self.held, self.target, self.sem = held, target, sem
        self.copy = pltpu.make_async_copy(held, target, sem)
        self.waited = False

    def __setitem__(self, at, value):
        self.held[at] = value

    def __getitem__(self, at):
        return self.held[at]

    def wait(self):
        self.copy.wait()
        self.waited = True

    def send(self, rows=None):
        if rows is None:
            self.copy.start()
        else:
            pltpu.make_async_copy(self.held.at[rows], self.target.at[rows], self.sem).start()


def call(
    kernel, ins, outs, name, near=(), scalars=(), bare=(), plain=None, scratch=(), parts=None,
    room=ALL, flops=0, moved=0,
):
    parts, plain = parts or {}, plain or {}
    away = [k for k in range(len(outs)) if k not in plain]
    far = [k for k in range(len(ins)) if k not in (*near, *scalars, *bare)]
    specs = [VMEM if k in near else SMEM if k in scalars else HBM for k in range(len(ins))]
    held = [pltpu.VMEM(ins[k].shape, ins[k].dtype) for k in far]
    held += [pltpu.VMEM(*outs[k]) for k in away]
    counts = [parts.get(k, 1) for k in far]
    dma = pltpu.SemaphoreType.DMA

    def body(*refs):
        operands, refs = list(refs[: len(ins)]), refs[len(ins) :]
        results, refs = list(refs[: len(outs)]), refs[len(outs) :]
        copies, refs = refs[: len(far)], refs[len(far) :]
        holds, refs = refs[: len(away)], refs[len(away) :]
        load_sems, store_sems = refs[0], refs[1]
        first = 0
        for k, copy, count in zip(far, copies, counts, strict=True):
            operands[k] = Loaded(operands[k], copy, load_sems, first, count)
            first += count
        for n, (k, hold) in enumerate(zip(away, holds, strict=True)):
            results[k] = Stored(hold, results[k], store_sems.at[n])
        kernel(*operands, *results, *refs[2:])
        for k in far:
            operands[k].wait()
        for k in away:
            if not results[k].waited:
                results[k].wait()

    return pl.pallas_call(
        body,
        out_shape=[jax.ShapeDtypeStruct(s, t) for s, t in outs],
        in_specs=specs,
        out_specs=[plain.get(k, HBM) for k in range(len(outs))],
        scratch_shapes=held + [dma((max(sum(counts), 1),)), dma((len(away),))] + list(scratch),
        compiler_params=pltpu.CompilerParams(vmem_limit_bytes=room),
        cost_estimate=pl.CostEstimate(flops=flops, bytes_accessed=moved, transcendentals=0),
        name=name,
    )(*ins)


def exchange(x):
    return lax.all_to_all(x, AXES, split_axis=0, concat_axis=0, tiled=True)


def local(features, cotangent, w_self, w_neigh, bias, src_slot, dst_slot, edge_live, mirror_list):
    line = mirror_list.reshape(1, MIRRORS)
    lists = mirror_list[0].T
    square = ((1024, 1024), BF16)
    payload = ((PEERS, 16, F), BF16)

    edges = (EDGES // LANES, LANES)
    src, dst = src_slot.reshape(edges), dst_slot.reshape(edges)
    rows_f32, rows_bf16 = ((1024, F), F32), ((1024, F), BF16)
    out1, code = call(
        pull_kernel,
        (edge_live, lists, src, dst, features),
        [payload, (edges, jnp.int32)],
        "pull",
        scalars=(0,),
        scratch=[pltpu.VMEM((32, EDGES), BF16), pltpu.VMEM((32, EDGES), BF16)],
    )
    got1 = exchange(out1)
    quarters = [pltpu.VMEM(*square), pltpu.VMEM(*square)]
    words, gm, gg, sums, flag, mm, mg = call(
        build_kernel,
        (edge_live, code, features),
        [
            ((2 * MASTERS, LANES), jnp.int32),
            square,
            square,
            rows_f32,
            ((1,), jnp.int32),
            square,
            square,
        ],
        "build",
        scalars=(0,),
        bare=(1,),
        plain={4: SMEM, 5: HBM, 6: HBM},
        scratch=[pltpu.SMEM(edges, jnp.int32), pltpu.SemaphoreType.DMA]
        + quarters
        + [pltpu.VMEM((WORDS, 1, LANES), jnp.int32) for _ in range(COPIES)],
        flops=20_000_000_000,
        moved=20_000_000,
    )
    (out2,) = call(
        push_kernel,
        (got1, sums, gg),
        [((PEERS, 8, F), BF16)],
        "push",
        near=(0,),
        room=55_400_000,
        parts={2: PARTS},
    )
    got2 = exchange(out2)
    turned, told, sums_m, tally = call(
        local_kernel,
        (flag, got1, features, words, mm, mg),
        [((F, MASTERS), BF16), rows_bf16, rows_f32, rows_bf16],
        "local",
        room=55_000_000,
        scalars=(0,),
        bare=(4, 5),
        scratch=quarters + [pltpu.SemaphoreType.DMA],
        flops=2_000_000_000,
        moved=6_000_000,
    )
    act, own, msg, out3, total = call(
        dense_kernel,
        (
            got2, line, told, tally, sums_m, features, w_self, w_neigh, bias.reshape(1, H),
            cotangent, turned,
        ),
        [((MASTERS, H), BF16), rows_f32, rows_f32, payload, ((8, F), F32)],
        "dense",
        near=(0,),
        room=55_000_000,
    )
    got3 = exchange(out3)
    turned_gg, mirror, base = call(
        back_local_kernel,
        (flag, gg, msg, words, own, mm, mg),
        [square, rows_f32, rows_f32],
        "back_local",
        scalars=(0,),
        bare=(5, 6),
        scratch=quarters + [pltpu.SemaphoreType.DMA],
        flops=2_000_000_000,
        moved=6_000_000,
    )
    (out4,) = call(
        back_push_kernel,
        (got3, mirror, total, turned_gg),
        [payload],
        "back_push",
        near=(0,),
        room=55_200_000,
        parts={3: PARTS},
    )
    got4 = exchange(out4)
    (base2,) = call(
        back_mirror_kernel,
        (got3, gm, base),
        [rows_f32],
        "back_mirror",
        room=55_000_000,
        flops=2_000_000_000,
        moved=6_000_000,
    )
    grad_features, grad_self, grad_neigh, bias_out = call(
        last_kernel,
        (line, got4, base2),
        [rows_bf16, ((F, H), F32), ((F, H), F32), ((2, F), F32)],
        "last",
        near=(1,),
        room=55_000_000,
    )
    return act, grad_features, grad_self, grad_neigh, bias_out.reshape(H)


def solution(mesh):
    placed = (
        P(AXES, None),
        P(AXES, None),
        P(),
        P(),
        P(),
        P(AXES),
        P(AXES),
        P(AXES),
        P(AXES, None, None),
    )
    return jax.shard_map(
        local,
        mesh=mesh,
        in_specs=placed,
        out_specs=(P(AXES, None), P(AXES, None), P(), P(), P()),
        check_vma=False,
    )
```
